32 devices in a mesh: rve: 4 (over z), gy: 2 (over x), gz: 4 (over y, core).
Axes of the slice: x: 2, y: 2, z: 4, core: 2. Of those that a mesh axis runs over, the one named last changes fastest.
Arguments:
- strain: float32 [32, 6], P('rve'), may hold values from -6 to 6
- tangent: float32 [32], P('rve'), may hold values from 0.5 to 2
- yield_list: int32 [16], P('rve'), may hold values from 0 to 7, as said below
- destination: int32 [16, 1], P('rve'), may hold values from 0 to 3; in each aligned block of 4 rows (0 to 3, 4 to 7, ...) at most 2 rows name the same one
- phase_map: int32 [4, 8, 32, 128], P('rve', 'gy', 'gz'), may hold values from 0 to 1
- polarization: float32 [4, 3, 6, 8, 32, 128], P('rve', None, None, 'gy', 'gz'), may hold values from -6 to 6
- stencil: float32 [3, 3, 27], replicated, may hold values from -0.6 to 3, as said below
Outputs:
- fields: float32 [4, 8, 3, 8, 32, 128], P('rve', None, None, 'gy', 'gz')
- stress_rows: float32 [16, 6], P('rve')
The draws below stay inside these ranges and needn't reach their ends.
Inputs may be any that keep to these rules, and one draw needn't show every extreme that they name: `yield_list`: the 4 entries of each macro device are distinct local point numbers, and each device lists 0 and 7. `destination`: among the 4 entries of one macro device, no group is named more than 2 times. stencil[c, d, o] equals stencil[d, c, 26 - o] for all channels and offsets.
All inputs are finite; a program needn't handle non-finite values.
Results may differ from the reference program's by a relative error of at most 0.0003.
Values sent between devices are 32-bit elements; how exact they have to be, the bound alone decides.
A program may use at most 192 MiB of HBM per device.

```python
import math
import jax
import jax.numpy as jnp
import numpy as np
from jax import lax

NX = 128
ROWS_DEV = 8
YLD = 4
CAP = 2
SWEEPS = 6
NY = 8
NZ = 32
LOADS = 8
MACRO = 32
YROWS = 16
N_RVE = 4


CENTRE_VALUE = 3.0


FACE_BASE = 0.085


FACE_ALONG = 0.1


EDGE_WEIGHT = 0.01


CORNER_WEIGHT = 0.004


CROSS_EDGE = 0.004


CROSS_CORNER = 0.002


def draw_stencil(key, part):
    offsets = jnp.arange(27, dtype=jnp.int32)
    components = jnp.stack([offsets // 9 - 1, offsets // 3 % 3 - 1, offsets % 3 - 1], axis=0).astype(jnp.float32)
    moving = jnp.abs(components[0]) + jnp.abs(components[1]) + jnp.abs(components[2])
    is_face = (moving == 1.0).astype(jnp.float32)
    is_edge = (moving == 2.0).astype(jnp.float32)
    is_corner = (moving == 3.0).astype(jnp.float32)
    same_channel = jnp.eye(3, dtype=jnp.float32)[:, :, None]
    along_channel = jnp.abs(components)
    own_part = -(FACE_BASE + FACE_ALONG * along_channel) * is_face[None, :] - EDGE_WEIGHT * is_edge[None, :] - CORNER_WEIGHT * is_corner[None, :]
    product = components[:, None, :] * components[None, :, :]
    cross_part = -(CROSS_EDGE * is_edge + CROSS_CORNER * is_corner)[None, None, :] * product * (1.0 - same_channel)
    pattern = same_channel * own_part[:, None, :] + cross_part
    raw_factors = jax.random.uniform(key, (3, 3, 27), jnp.float32, 0.85, 1.0)
    factors = 0.5 * (raw_factors + jnp.transpose(raw_factors, (1, 0, 2))[:, :, ::-1])
    centre = same_channel * (offsets == 13).astype(jnp.float32)[None, None, :]
    return CENTRE_VALUE * (pattern * factors + centre)


def draw_yield_list(key, part):
    block_count = YROWS // YLD
    block_keys = jax.random.split(key, block_count)

    def one_block(block_key):
        first_key, second_key = jax.random.split(block_key)
        middle = 1 + jax.random.permutation(first_key, ROWS_DEV - 2)[:YLD - 2]
        chosen = jnp.concatenate([jnp.array([0, ROWS_DEV - 1], dtype=jnp.int32), middle.astype(jnp.int32)])
        return chosen[jax.random.permutation(second_key, YLD)]
    return jax.vmap(one_block)(block_keys).reshape(YROWS).astype(jnp.int32)


def plant(drawn, rng, least, high):
    place = [jax.random.randint(jax.random.fold_in(rng, axis), (), 0, length) for axis, length in enumerate(drawn.shape)]
    widest = drawn.shape.index(max(drawn.shape))
    next_to = place[:widest] + [(place[widest] + 1) % drawn.shape[widest]] + place[widest + 1:]
    return drawn.at[tuple(place)].set(least).at[tuple(next_to)].set(high)


def block_levels(rng, shape, cuts, low, high):
    factor_of = 1.0
    for position, blocks in cuts:
        steps = jax.random.uniform(jax.random.fold_in(jax.random.fold_in(rng, 6), position), (blocks,), jnp.float32, low / len(cuts), high / len(cuts))
        factor_of = factor_of * jnp.repeat(jnp.exp(steps), shape[position] // blocks).reshape((-1,) + (1,) * (len(shape) - 1 - position))
    return factor_of


def assign_block(own_key, own, number, rows, number_of, top, reach, slope):
    order = jax.random.permutation(own_key, number_of)
    crowded, usual = shares(number_of, rows * top, reach, slope, True), shares(number_of, rows * top, reach, slope, False)
    places = jnp.arange(number_of)

    def named(tallies, rotation):
        used = int((tallies > 0).sum())
        fixed = max(1, used // 4)
        passed = fixed + (places - fixed + rotation * (used - fixed)) % max(1, number_of - fixed)
        return jnp.zeros((number_of,), jnp.int32).at[order[jnp.where(places < fixed, places, passed)]].set(jnp.asarray(tallies, jnp.int32))

    tallies = jnp.where(number % 4 == 0, named(crowded, number // 4), named(usual, number - number // 4 - 1))
    mixed = jax.random.permutation(jax.random.fold_in(own, 3), number_of)
    giver, receiver = mixed[0:number_of // 2 * 2:2], mixed[1:number_of // 2 * 2:2]
    margin = jnp.minimum(tallies[giver] - 1, reach - tallies[receiver]) // 2
    margin = jnp.where((giver == order[0]) | (receiver == order[0]) | (tallies[receiver] == 0), 0, jnp.maximum(margin, 0))
    passed = jax.random.randint(jax.random.fold_in(own, 4), (number_of // 2,), 0, 1 << 20) % (margin + 1)
    tallies = tallies.at[giver].add(-passed).at[receiver].add(passed)
    labels = jnp.searchsorted(jnp.cumsum(tallies), jnp.arange(rows * top), side="right").astype(jnp.int32)
    grid = labels.reshape(top, rows).T
    grid = grid[jax.random.permutation(jax.random.fold_in(own, 1), rows)]
    rotation = jax.random.randint(jax.random.fold_in(own, 2), (rows, 1), 0, top)
    return jnp.take_along_axis(grid, (jnp.arange(top)[None, :] + rotation) % top, axis=1)


def shares(count, total, reach, slope, full):
    portions = [(1 << 20) // math.isqrt(standing ** slope) + 1 for standing in range(1, count + 1)]
    largest = reach if full else min(reach, max(-(-total // count), total * portions[0] // sum(portions)))
    least = 1 if total - largest >= count - 1 else 0
    counts, spare = [largest] + [least] * (count - 1), total - largest - least * (count - 1)
    while spare > 0:
        candidates = [i for i in range(1, count) if counts[i] < largest] or [i for i in range(1, count) if counts[i] < reach]
        mass, budget = sum([portions[i] for i in candidates]), spare
        for i in candidates:
            extra = min(reach - counts[i], max(1, budget * portions[i] // mass), spare)
            counts[i] = counts[i] + extra
            spare = spare - extra
    return np.array(counts)


def noise(rng, extent, deviation, reach, cuts=(), kind=jnp.bfloat16):
    drawn = deviation * jax.random.normal(rng, extent, jnp.float32)
    if cuts:
        drawn = drawn * block_levels(rng, extent, cuts, -0.22, 0.18)
    return jnp.clip(drawn, -reach, reach).astype(kind)


def setup_inputs(seed: int = 0) -> dict:
    seeds = jax.random.split(jax.random.key(seed), 8)
    strain = noise(seeds[0], (MACRO, 6), 1.0, 6.0, ((0, 4),), jnp.float32)
    tangent = jnp.clip(jnp.exp(math.log(2.0) - 1.3862944 * jax.random.uniform(seeds[1], (MACRO,), jnp.float32) ** block_levels(seeds[1], (MACRO,), ((0, 4),), -0.2, 0.2)), 0.5, 2.0)
    yield_list = draw_yield_list(jax.random.fold_in(seeds[7], 71), 0)
    destination_keys = jax.random.split(jax.random.fold_in(seeds[3], 1), YROWS // YLD)
    destination_turns = jax.random.permutation(jax.random.fold_in(seeds[3], 3), YROWS // YLD)
    destination = jax.vmap(lambda own, number: assign_block(jax.random.fold_in(seeds[3], 2), own, number, YLD, N_RVE, 1, CAP, 2))(destination_keys, destination_turns).reshape((YROWS, 1))
    phase_map = plant(jax.random.randint(seeds[4], (N_RVE, NY, NZ, NX), 0, 2), jax.random.fold_in(seeds[4], 1), 0, 1).astype(jnp.int32)
    polarization = noise(seeds[5], (N_RVE, 3, 6, NY, NZ, NX), 1.0, 6.0, ((0, 4), (3, 2), (4, 4)), jnp.float32)
    stencil = draw_stencil(jax.random.fold_in(seeds[7], 71), 0)
    return dict(strain=strain, tangent=tangent, yield_list=yield_list, destination=destination, phase_map=phase_map, polarization=polarization, stencil=stencil)


FULL_PRECISION = lax.Precision.HIGHEST
LOWER_BOUND = 0.05
UPPER_BOUND = 1.95


def chebyshev_weights(sweep_count):
    centre_value = 0.5 * (UPPER_BOUND + LOWER_BOUND)
    half_width = 0.5 * (UPPER_BOUND - LOWER_BOUND)
    ratio_value = centre_value / half_width
    rho_before = 1.0 / ratio_value
    weights = []
    for sweep_index in range(1, sweep_count):
        rho_after = 1.0 / (2.0 * ratio_value - rho_before)
        weights.append((rho_after * rho_before, 2.0 * rho_after / half_width))
        rho_before = rho_after
    return 1.0 / centre_value, weights


def apply_stiffness(field_now, moduli, stencil):
    inner_y = field_now.shape[2] - 2
    inner_z = field_now.shape[3] - 2
    centre_mod = moduli[:, 1:1 + inner_y, 1:1 + inner_z, :]
    running = None
    for shift_y in (-1, 0, 1):
        for shift_z in (-1, 0, 1):
            shifted = field_now[:, :, 1 + shift_y:1 + shift_y + inner_y, 1 + shift_z:1 + shift_z + inner_z, :]
            shifted_mod = moduli[:, 1 + shift_y:1 + shift_y + inner_y, 1 + shift_z:1 + shift_z + inner_z, :]
            for shift_x in (-1, 0, 1):
                if shift_x != 0:
                    rolled = jnp.roll(shifted, -shift_x, axis=4)
                    rolled_mod = jnp.roll(shifted_mod, -shift_x, axis=3)
                else:
                    rolled = shifted
                    rolled_mod = shifted_mod
                offset_index = (shift_y + 1) * 9 + (shift_z + 1) * 3 + (shift_x + 1)
                edge_mod = 0.5 * (centre_mod + rolled_mod)
                contrib = jnp.einsum("cd,ldyzx->lcyzx", stencil[:, :, offset_index], edge_mod[:, None] * rolled, precision=FULL_PRECISION)
                running = contrib if running is None else running + contrib
    return running


def solve_group(phase_group, polar_group, strain_group, tangent_group, stencil):
    moduli = jnp.where(phase_group[None] == 1, tangent_group[:, None, None, None], jnp.float32(1.0))
    body_force = moduli[:, None] * jnp.einsum("cjyzx,lj->lcyzx", polar_group, strain_group, precision=FULL_PRECISION)
    centre_diag = jnp.diagonal(stencil[:, :, 13])
    inverse_diag = 1.0 / (centre_diag[None, :, None, None, None] * moduli[:, None])
    wrapped_mod = jnp.pad(moduli, ((0, 0), (1, 1), (1, 1), (0, 0)), mode="wrap")
    first_weight, weights = chebyshev_weights(SWEEPS)
    update = first_weight * (body_force * inverse_diag)
    field_now = update
    for old_weight, new_weight in weights:
        wrapped = jnp.pad(field_now, ((0, 0), (0, 0), (1, 1), (1, 1), (0, 0)), mode="wrap")
        residual_now = body_force - apply_stiffness(wrapped, wrapped_mod, stencil)
        update = old_weight * update + new_weight * (residual_now * inverse_diag)
        field_now = field_now + update
    coupled = jnp.einsum("cjyzx,lcyzx->lj", polar_group, moduli[:, None] * field_now, precision=FULL_PRECISION)
    stress = (coupled + strain_group * jnp.sum(moduli, axis=(1, 2, 3))[:, None]) / (NY * NZ * NX)
    return field_now, stress


def reference(strain, tangent, yield_list, destination, phase_map, polarization, stencil):
    rows_index = jnp.arange(YROWS, dtype=jnp.int32)
    sender = rows_index // YLD
    group_of = destination[:, 0]
    earlier = (group_of[:, None] == group_of[None, :]) & (sender[:, None] == sender[None, :]) & (rows_index[None, :] < rows_index[:, None])
    rank_in = jnp.sum(earlier.astype(jnp.int32), axis=1)
    slot_of = sender * CAP + rank_in
    group_ids = jnp.arange(N_RVE, dtype=jnp.int32)
    slot_ids = jnp.arange(LOADS, dtype=jnp.int32)
    onehot = ((group_of[None, None, :] == group_ids[:, None, None]) & (slot_of[None, None, :] == slot_ids[None, :, None])).astype(jnp.float32)
    source = sender * ROWS_DEV + yield_list
    picker = (jnp.arange(MACRO, dtype=jnp.int32)[None, :] == source[:, None]).astype(jnp.float32)
    row_strain = jnp.dot(picker, strain, precision=FULL_PRECISION)
    row_tangent = jnp.dot(picker, tangent, precision=FULL_PRECISION)
    slot_strain = jnp.einsum("gli,ij->glj", onehot, row_strain, precision=FULL_PRECISION)
    slot_tangent = jnp.einsum("gli,i->gl", onehot, row_tangent, precision=FULL_PRECISION) + 1.0 - jnp.sum(onehot, axis=2)

    def one_group(packed):
        return solve_group(packed[0], packed[1], packed[2], packed[3], stencil)

    fields, stresses = lax.map(one_group, (phase_map, polarization, slot_strain, slot_tangent))
    stress_rows = jnp.einsum("gli,glj->ij", onehot, stresses, precision=FULL_PRECISION)
    return fields, stress_rows
```

```python
import functools

import jax
import jax.numpy as jnp
from jax import lax
from jax.experimental import pallas as pl
from jax.experimental.pallas import tpu as pltpu
from jax.sharding import PartitionSpec as P

CAP = 2
SWEEPS = 6
MESH = pl.DeviceIdType.MESH
TANGENT, TARGET, RANK, LISTED = 6, 7, 8, 9


FULL_PRECISION = lax.Precision.HIGHEST
LOWER_BOUND = 0.05
UPPER_BOUND = 1.95


def padded(block, sides, width):
    for axis, dim in sides:
        count = lax.axis_size(axis)
        forward = [(i, i + 1) for i in range(count - 1)]
        forward.append((count - 1, 0))
        backward = [(target, source) for source, target in forward]
        low = lax.ppermute(
            lax.slice_in_dim(block, block.shape[dim] - width, None, axis=dim), axis, forward
        )
        high = lax.ppermute(lax.slice_in_dim(block, 0, width, axis=dim), axis, backward)
        block = jnp.concatenate([low, block, high], axis=dim)
    return block


def chebyshev_weights(sweep_count):
    centre_value = 0.5 * (UPPER_BOUND + LOWER_BOUND)
    half_width = 0.5 * (UPPER_BOUND - LOWER_BOUND)
    ratio_value = centre_value / half_width
    rho_before = 1.0 / ratio_value
    weights = []
    for sweep_index in range(1, sweep_count):
        rho_after = 1.0 / (2.0 * ratio_value - rho_before)
        weights.append((rho_after * rho_before, 2.0 * rho_after / half_width))
        rho_before = rho_after
    return (1.0 / centre_value, weights)


def trim_margin(values_in, margin_have, margin_want, first_dim):
    excess = margin_have - margin_want
    values_in = lax.slice_in_dim(
        values_in, excess, values_in.shape[first_dim] - excess, axis=first_dim
    )
    return lax.slice_in_dim(
        values_in, excess, values_in.shape[first_dim + 1] - excess, axis=first_dim + 1
    )


def apply_stiffness(field_now, moduli, stencil):
    inner_y = field_now.shape[2] - 2
    inner_z = field_now.shape[3] - 2
    centre_mod = moduli[:, 1 : 1 + inner_y, 1 : 1 + inner_z, :]
    running = [None, None, None]
    for shift_y in (-1, 0, 1):
        for shift_z in (-1, 0, 1):
            shifted = field_now[
                :, :, 1 + shift_y : 1 + shift_y + inner_y, 1 + shift_z : 1 + shift_z + inner_z, :
            ]
            shifted_mod = moduli[
                :, 1 + shift_y : 1 + shift_y + inner_y, 1 + shift_z : 1 + shift_z + inner_z, :
            ]
            for shift_x in (-1, 0, 1):
                if shift_x != 0:
                    rolled = jnp.roll(shifted, -shift_x, axis=4)
                    rolled_mod = jnp.roll(shifted_mod, -shift_x, axis=3)
                else:
                    rolled = shifted
                    rolled_mod = shifted_mod
                offset_index = (shift_y + 1) * 9 + (shift_z + 1) * 3 + (shift_x + 1)
                edge_mod = 0.5 * (centre_mod + rolled_mod)
                weighted = [edge_mod * rolled[:, channel_in] for channel_in in range(3)]
                for channel_out in range(3):
                    mixed = stencil[channel_out, 0, offset_index] * weighted[0]
                    mixed = mixed + stencil[channel_out, 1, offset_index] * weighted[1]
                    mixed = mixed + stencil[channel_out, 2, offset_index] * weighted[2]
                    if running[channel_out] is None:
                        running[channel_out] = mixed
                    else:
                        running[channel_out] = running[channel_out] + mixed
    return jnp.stack(running, axis=1)


def body(strain, tangent, yield_list, destination, phase_map, polarization, stencil):
    groups = lax.axis_size("rve")
    rows_here = strain.shape[0]
    yield_count = yield_list.shape[0]
    picker = (jnp.arange(rows_here, dtype=jnp.int32)[None, :] == yield_list[:, None]).astype(
        jnp.float32
    )
    row_strain = jnp.dot(picker, strain, precision=FULL_PRECISION)
    row_tangent = jnp.dot(picker, tangent, precision=FULL_PRECISION)
    target = destination[:, 0]
    positions = jnp.arange(yield_count, dtype=jnp.int32)
    earlier = (target[:, None] == target[None, :]) & (positions[None, :] < positions[:, None])
    rank_in = jnp.sum(earlier.astype(jnp.int32), axis=1)
    group_ids = jnp.arange(groups, dtype=jnp.int32)
    slot_ids = jnp.arange(CAP, dtype=jnp.int32)
    onehot = (
        (target[None, None, :] == group_ids[:, None, None])
        & (rank_in[None, None, :] == slot_ids[None, :, None])
    ).astype(jnp.float32)
    packet = jnp.einsum("gci,ij->gcj", onehot, row_strain, precision=FULL_PRECISION)
    packet_tangent = (
        jnp.einsum("gci,i->gc", onehot, row_tangent, precision=FULL_PRECISION)
        + 1.0
        - jnp.sum(onehot, axis=2)
    )
    parcel = jnp.concatenate([packet, packet_tangent[:, :, None]], axis=2)
    arrived = lax.all_to_all(parcel, "rve", split_axis=0, concat_axis=0, tiled=True)
    slot_strain = arrived[:, :, :6].reshape(groups * CAP, 6)
    slot_tangent = arrived[:, :, 6].reshape(groups * CAP)
    phase_wide = padded(phase_map[0], (("gy", 0), ("gz", 1)), 2)
    moduli_wide = jnp.where(
        phase_wide[None] == 1, slot_tangent[:, None, None, None], jnp.float32(1.0)
    )
    moduli_core = trim_margin(moduli_wide, 2, 0, 1)
    moduli_one = trim_margin(moduli_wide, 2, 1, 1)
    polar_local = polarization[0]
    centre_diag = jnp.diagonal(stencil[:, :, 13])
    body_force = moduli_core[:, None] * jnp.einsum(
        "cjyzx,lj->lcyzx", polar_local, slot_strain, precision=FULL_PRECISION
    )
    inverse_diag = 1.0 / (centre_diag[None, :, None, None, None] * moduli_core[:, None])
    first_weight, weights = chebyshev_weights(SWEEPS)
    update = first_weight * (body_force * inverse_diag)
    field_now = update
    for old_weight, new_weight in weights:
        wrapped = padded(field_now, (("gy", 2), ("gz", 3)), 1)
        residual_now = body_force - apply_stiffness(wrapped, moduli_one, stencil)
        update = old_weight * update + new_weight * (residual_now * inverse_diag)
        field_now = field_now + update
    coupled = jnp.einsum(
        "cjyzx,lcyzx->lj", polar_local, moduli_core[:, None] * field_now, precision=FULL_PRECISION
    )
    partial_value = coupled + slot_strain * jnp.sum(moduli_core, axis=(1, 2, 3))[:, None]
    total_cells = (
        lax.axis_size("gy")
        * lax.axis_size("gz")
        * field_now.shape[2]
        * field_now.shape[3]
        * field_now.shape[4]
    )
    summed = lax.psum(partial_value, ("gy", "gz")) / total_cells
    returned = lax.all_to_all(
        summed.reshape(groups, CAP, 6), "rve", split_axis=0, concat_axis=0, tiled=True
    )
    stress_rows = jnp.einsum("gci,gcj->ij", onehot, returned, precision=FULL_PRECISION)
    return (field_now[None], stress_rows)


def kernel(
    groups, ngy, ngz,
    strain, tangent, yield_list, destination, stencil, phase, polar,
    fields, rows_out,
    tables, slots, phase_all, force_out, force, matrix, spread, field_now, update,
    mod_mid, mod_low, mod_high, mod_inv, sums, partials, totals,
    table_send, table_recv, phase_send, phase_recv, force_send, force_recv,
    field_send, field_recv, part_send, part_recv, total_send, total_recv,
):
    f32, bf16 = jnp.float32, jnp.bfloat16
    channels, strains = polar.shape[1], polar.shape[2]
    y_here, z_here, nx = polar.shape[3:]
    ny, nz = y_here * ngy, z_here * ngz
    wide = channels * nz
    slot_rows = 3 * wide
    depth = 3 * slot_rows
    listed = yield_list.shape[0]
    loads = groups * CAP
    my_r, my_y, my_z = lax.axis_index("rve"), lax.axis_index("gy"), lax.axis_index("gz")
    my_load = my_y * ngz + my_z

    def turned(base, step, count):
        return lax.rem(base + step + count, count)

    mates = [(dy, dz) for dy in list(range(1, ngy)) + [0] for dz in list(range(1, ngz)) + [0]]
    others = [mate for mate in mates if mate != (0, 0)]

    def mate_id(dy, dz):
        return {"gy": turned(my_y, dy, ngy), "gz": turned(my_z, dz, ngz)}

    def block(dy, dz):
        y_at = turned(my_y, dy, ngy) * y_here
        z_at = pl.multiple_of(turned(my_z, dz, ngz) * z_here, 8)
        return pl.ds(y_at, y_here), pl.ds(z_at, z_here)

    barrier = pltpu.get_barrier_semaphore()
    for dy, dz in others:
        pl.semaphore_signal(barrier, inc=1, device_id=mate_id(dy, dz), device_id_type=MESH)
    for step in range(1, groups):
        pl.semaphore_signal(
            barrier, inc=1, device_id={"rve": turned(my_r, step, groups)}, device_id_type=MESH
        )

    row_ids = lax.broadcasted_iota(jnp.int32, (8, 128), 0)
    lane_ids = lax.broadcasted_iota(jnp.int32, (8, 128), 1)
    table = jnp.zeros((8, 128), f32)
    for i in range(listed):
        point, target = yield_list[i], destination[i, 0]
        rank = jnp.int32(0)
        for k in range(i):
            rank = rank + jnp.where(destination[k, 0] == target, 1, 0)
        values = [strain[point, j] for j in range(strains)]
        values += [tangent[point], target.astype(f32), rank.astype(f32), jnp.float32(1.0)]
        for j, value in enumerate(values):
            table = jnp.where((row_ids == i) & (lane_ids == j), value, table)
    tables[my_r] = table

    pl.semaphore_wait(barrier, len(others) + groups - 1)

    def table_copy(step, owner):
        return pltpu.make_async_remote_copy(
            src_ref=tables.at[my_r], dst_ref=tables.at[owner],
            send_sem=table_send.at[step], recv_sem=table_recv.at[step],
            device_id={"rve": turned(my_r, step, groups)}, device_id_type=MESH,
        )

    def phase_copy(index, dy, dz):
        y_at, z_at = block(dy, dz)
        to_y, to_z = others[index]
        return pltpu.make_async_remote_copy(
            src_ref=phase.at[0], dst_ref=phase_all.at[y_at, z_at],
            send_sem=phase_send.at[index], recv_sem=phase_recv.at[index],
            device_id=mate_id(to_y, to_z), device_id_type=MESH,
        )

    for step in range(1, groups):
        table_copy(step, my_r).start()
    for index in range(len(others)):
        phase_copy(index, 0, 0).start()
    own_y, own_z = block(0, 0)
    phase_all[own_y, own_z, :] = phase[0]

    column = lax.broadcasted_iota(jnp.int32, (1, depth), 1)
    column_y = column // slot_rows
    column_kind = lax.rem(column, slot_rows) // wide
    column_d = lax.rem(column, wide) // nz
    picks = [[(column_y == dy) & (column_d == d) for d in range(channels)] for dy in range(3)]
    z_row = lax.broadcasted_iota(jnp.int32, (nz, depth), 0)
    z_column = lax.rem(lax.broadcasted_iota(jnp.int32, (nz, depth), 1), nz)
    bands = [z_column == lax.rem(z_row + dz - 1 + nz, nz) for dz in range(3)]
    is_low = jnp.broadcast_to(column_kind, (nz, depth)) == 1
    for dx in range(3):
        for c in range(channels):
            values = jnp.zeros((nz, depth), f32)
            for dz in range(3):
                line = jnp.zeros((1, depth), f32)
                for dy in range(3):
                    for d in range(channels):
                        line = jnp.where(
                            picks[dy][d], 0.5 * stencil[c, d, dy * 9 + dz * 3 + dx], line
                        )
                values = values + jnp.where(bands[dz], line, 0.0)
            high = values.astype(bf16).astype(f32)
            low = values - high
            at = (dx * channels + c) * nz
            matrix[at : at + nz, :] = jnp.where(is_low, low, high).astype(bf16)

    for step in range(1, groups):
        table_copy(step, turned(my_r, -step, groups)).wait_recv()
    for source in range(groups):
        heard = tables[source]
        named = (heard[:, TARGET : TARGET + 1] == my_r.astype(f32)) & (
            heard[:, LISTED : LISTED + 1] == 1.0
        )
        for rank in range(CAP):
            chosen = named & (heard[:, RANK : RANK + 1] == float(rank))
            line = jnp.sum(jnp.where(chosen, heard, 0.0), axis=0, keepdims=True)
            missing = 1.0 - line[:, LISTED : LISTED + 1]
            line = line + jnp.where(lane_ids[:1] == TANGENT, missing, 0.0)
            at = source * CAP + rank
            slots[at : at + 1, :] = line

    def slot_value(load, index):
        return jnp.broadcast_to(slots[pl.ds(load, 1), :][:, index : index + 1], (8, 128))

    def force_copy(index, dy, dz):
        y_at, z_at = block(dy, dz)
        return pltpu.make_async_remote_copy(
            src_ref=force_out.at[index], dst_ref=force.at[:, y_at, z_at],
            send_sem=force_send.at[index], recv_sem=force_recv.at[index],
            device_id=mate_id(*others[index]), device_id_type=MESH,
        )

    for index, (dy, dz) in enumerate(mates):
        load = turned(my_y, dy, ngy) * ngz + turned(my_z, dz, ngz)
        strain_of = [slot_value(load, j) for j in range(strains)]
        for c in range(channels):
            for y in range(y_here):
                value = polar[0, c, 0, y] * strain_of[0]
                for j in range(1, strains):
                    value = value + polar[0, c, j, y] * strain_of[j]
                if (dy, dz) == (0, 0):
                    force[c, my_y * y_here + y, own_z, :] = value
                else:
                    force_out[index, c, y] = value
        if (dy, dz) != (0, 0):
            force_copy(index, 0, 0).start()

    for index, (dy, dz) in enumerate(others):
        phase_copy(index, -dy, -dz).wait_recv()
    tangent_row = slots[pl.ds(my_load, 1), :][:, TANGENT : TANGENT + 1]
    my_tangent = jnp.broadcast_to(tangent_row, (nz, nx))
    inverse_tangent = 1.0 / my_tangent
    for y in range(ny):
        second = phase_all[y] == 1
        mod = jnp.where(second, my_tangent, 1.0)
        mod_mid[y] = mod
        mod_low[y] = pltpu.roll(mod, nx - 1, 1)
        mod_high[y] = pltpu.roll(mod, 1, 1)
        mod_inv[y] = jnp.where(second, inverse_tangent, 1.0)
    ones = jnp.ones((nz, nx), f32)
    inverse_centre = [1.0 / (ones * stencil[c, c, 13]) for c in range(channels)]

    def put(buffer, y, c, value):
        both = jnp.concatenate([value, value * mod_mid[y]], axis=1)
        high = both.astype(bf16)
        low = (both - high.astype(f32)).astype(bf16)
        at = pl.multiple_of((y + 1) * slot_rows + c * nz, 16)
        spread[buffer, pl.ds(at, nz), :] = high
        spread[buffer, pl.ds(at + wide, nz), :] = high
        spread[buffer, pl.ds(at + 2 * wide, nz), :] = low

    def wrap(buffer):
        spread[buffer, 0:slot_rows, :] = spread[buffer, ny * slot_rows : (ny + 1) * slot_rows, :]
        spread[buffer, (ny + 1) * slot_rows : (ny + 2) * slot_rows, :] = spread[
            buffer, slot_rows : 2 * slot_rows, :
        ]

    for index, (dy, dz) in enumerate(others):
        force_copy(index, -dy, -dz).wait_recv()
    first_weight, weights = chebyshev_weights(SWEEPS)
    for y in range(ny):
        for c in range(channels):
            value = first_weight * (force[c, y] * inverse_centre[c])
            update[c, y] = value
            field_now[c, y] = value
            put(0, y, c, value)
    wrap(0)

    def sweep_row(buffer, y, old_weight, new_weight, last):
        at = y * slot_rows if isinstance(y, int) else pl.multiple_of(y * slot_rows, 16)
        product = jnp.dot(
            matrix[...], spread[buffer, pl.ds(at, depth), :], preferred_element_type=f32
        )
        for c in range(channels):
            parts = []
            for dx, mod in enumerate((mod_low, mod_mid, mod_high)):
                row = (dx * channels + c) * nz
                parts.append(
                    mod[y] * product[row : row + nz, :nx] + product[row : row + nz, nx:]
                )
            stiff = parts[1] + pltpu.roll(parts[0], 1, 1) + pltpu.roll(parts[2], nx - 1, 1)
            residual = (force[c, y] - stiff * mod_inv[y]) * inverse_centre[c]
            step = old_weight * update[c, y] + new_weight * residual
            value = field_now[c, y] + step
            field_now[c, y] = value
            if not last:
                update[c, y] = step
                put(1 - buffer, y, c, value)

    def sweep(k, carry):
        old_weight, new_weight = jnp.float32(weights[0][0]), jnp.float32(weights[0][1])
        for position in range(1, len(weights) - 1):
            old_weight = jnp.where(k == position, weights[position][0], old_weight)
            new_weight = jnp.where(k == position, weights[position][1], new_weight)
        buffer = lax.rem(k, 2)
        for y in range(ny):
            sweep_row(buffer, y, old_weight, new_weight, False)
        wrap(1 - buffer)
        return carry

    lax.fori_loop(0, len(weights) - 1, sweep, 0)

    def field_copy(dy, dz, y, load):
        to_y, to_z = turned(my_y, dy, ngy), turned(my_z, dz, ngz)
        z_at = pl.ds(pl.multiple_of(to_z * z_here, 8), z_here)
        return pltpu.make_async_remote_copy(
            src_ref=field_now.at[:, to_y * y_here + y, z_at],
            dst_ref=fields.at[0, load, :, y],
            send_sem=field_send.at[dy, dz, y], recv_sem=field_recv.at[dy, dz, y],
            device_id={"gy": to_y, "gz": to_z}, device_id_type=MESH,
        )

    final_buffer = (len(weights) - 1) % 2
    for dy in list(range(1, ngy)) + [0]:
        for y in range(y_here):
            row = turned(my_y, dy, ngy) * y_here + y
            sweep_row(final_buffer, row, weights[-1][0], weights[-1][1], True)
            for dz in list(range(1, ngz)) + [0]:
                if (dy, dz) != (0, 0):
                    field_copy(dy, dz, y, my_load).start()
                else:
                    for c in range(channels):
                        fields[0, my_load, c, y] = field_now[c, row, own_z, :]

    seconds = [phase[0, y] == 1 for y in range(y_here)]
    for dy, dz in mates:
        load = turned(my_y, -dy, ngy) * ngz + turned(my_z, -dz, ngz)
        if (dy, dz) != (0, 0):
            for y in range(y_here):
                field_copy(dy, dz, y, load).wait_recv()
        slope = slot_value(load, TANGENT)
        totals_of = [jnp.zeros((8, 128), f32) for _ in range(strains)]
        for y in range(y_here):
            mod = jnp.where(seconds[y], slope, 1.0)
            for c in range(channels):
                flux = mod * fields[0, load, c, y]
                for j in range(strains):
                    totals_of[j] = totals_of[j] + polar[0, c, j, y] * flux
        for j in range(strains):
            sums[j, pl.ds(load, 1), :] = jnp.sum(totals_of[j], axis=0, keepdims=True)
    ones_here = jnp.zeros((8, 128), f32)
    for y in range(y_here):
        ones_here = ones_here + jnp.where(seconds[y], 1.0, 0.0)
    second_count = jnp.sum(jnp.sum(ones_here, axis=0, keepdims=True), axis=1, keepdims=True)
    slot_table = slots[...]
    mod_sum = second_count * slot_table[:, TANGENT : TANGENT + 1] + (
        float(y_here * z_here * nx) - second_count
    )
    share = jnp.where(lane_ids < strains, slot_table * mod_sum, 0.0)
    for j in range(strains):
        share = share + jnp.where(
            lane_ids == j, jnp.sum(sums[j], axis=1, keepdims=True), 0.0
        )
    partials[len(others)] = share * (1.0 / (ny * nz * nx))

    def part_copy(index):
        return pltpu.make_async_remote_copy(
            src_ref=partials.at[len(others)], dst_ref=partials.at[index],
            send_sem=part_send.at[index], recv_sem=part_recv.at[index],
            device_id=mate_id(*others[index]), device_id_type=MESH,
        )

    for index in range(len(others)):
        part_copy(index).start()
    for index in range(len(others)):
        part_copy(index).wait_recv()
    total = partials[0]
    for index in range(1, len(mates)):
        total = total + partials[index]
    totals[my_r] = total

    def total_copy(step, owner):
        return pltpu.make_async_remote_copy(
            src_ref=totals.at[my_r], dst_ref=totals.at[owner],
            send_sem=total_send.at[step], recv_sem=total_recv.at[step],
            device_id={"rve": turned(my_r, step, groups)}, device_id_type=MESH,
        )

    for step in range(1, groups):
        total_copy(step, my_r).start()
    for step in range(1, groups):
        total_copy(step, turned(my_r, -step, groups)).wait_recv()
    mine = tables[my_r]
    answer = jnp.zeros((8, 128), f32)
    for group in range(groups):
        for rank in range(CAP):
            chosen = (mine[:, TARGET : TARGET + 1] == float(group)) & (
                mine[:, RANK : RANK + 1] == float(rank)
            )
            line = totals[group, pl.ds(my_r * CAP + rank, 1), :]
            answer = answer + jnp.where(chosen, line, 0.0)
    rows_out[...] = answer[:listed, :strains]

    for step in range(1, groups):
        table_copy(step, my_r).wait_send()
        total_copy(step, my_r).wait_send()
    for index, (dy, dz) in enumerate(others):
        phase_copy(index, 0, 0).wait_send()
        force_copy(index, 0, 0).wait_send()
        part_copy(index).wait_send()
        for y in range(y_here):
            field_copy(dy, dz, y, my_load).wait_send()


def fused_body(strain, tangent, yield_list, destination, phase_map, polarization, stencil):
    groups, ngy, ngz = (lax.axis_size(name) for name in ("rve", "gy", "gz"))
    channels = polarization.shape[1]
    strains = polarization.shape[2]
    y_here, z_here, nx = polarization.shape[3:]
    ny, nz = y_here * ngy, z_here * ngz
    loads = groups * CAP
    count = ngy * ngz
    f32 = jnp.float32
    slot_rows = 3 * channels * nz
    vmem = pl.BlockSpec(memory_space=pltpu.VMEM)
    smem = pl.BlockSpec(memory_space=pltpu.SMEM)
    cell = pltpu.VMEM((ny, nz, nx), f32)
    vector = pltpu.VMEM((channels, ny, nz, nx), f32)

    def dma(*shape):
        return pltpu.SemaphoreType.DMA(shape)

    return pl.pallas_call(
        functools.partial(kernel, groups, ngy, ngz),
        out_shape=(
            jax.ShapeDtypeStruct((1, loads, channels, y_here, z_here, nx), f32),
            jax.ShapeDtypeStruct((yield_list.shape[0], strains), f32),
        ),
        in_specs=[smem, smem, smem, smem, smem, vmem, vmem],
        out_specs=(vmem, vmem),
        scratch_shapes=[
            pltpu.VMEM((groups, 8, 128), f32),
            pltpu.VMEM((loads, 128), f32),
            pltpu.VMEM((ny, nz, nx), jnp.int32),
            pltpu.VMEM((count, channels, y_here, z_here, nx), f32),
            vector,
            pltpu.VMEM((3 * channels * nz, 3 * slot_rows), jnp.bfloat16),
            pltpu.VMEM((2, (ny + 2) * slot_rows, 2 * nx), jnp.bfloat16),
            vector,
            vector,
            cell, cell, cell, cell,
            pltpu.VMEM((strains, loads, 128), f32),
            pltpu.VMEM((count, 8, 128), f32),
            pltpu.VMEM((groups, 8, 128), f32),
            dma(groups), dma(groups), dma(count), dma(count), dma(count), dma(count),
            dma(ngy, ngz, y_here), dma(ngy, ngz, y_here),
            dma(count), dma(count), dma(groups), dma(groups),
        ],
        compiler_params=pltpu.CompilerParams(
            collective_id=0, has_side_effects=True, vmem_limit_bytes=40 * 1024 * 1024
        ),
    )(strain, tangent, yield_list, destination, stencil, phase_map, polarization)


def body_for(mesh):
    def chosen(*arguments):
        strain, _, yield_list, _, phase_map, _, _ = arguments
        loads = lax.axis_size("rve") * CAP
        one_load_each = lax.axis_size("gy") * lax.axis_size("gz") == loads
        tiled = phase_map.shape[2] == 8 and phase_map.shape[3] == 128 and loads == 8
        if one_load_each and tiled and yield_list.shape[0] <= 8:
            return fused_body(*arguments)
        return body(*arguments)

    return chosen


def solution(mesh):
    return jax.shard_map(
        body_for(mesh),
        mesh=mesh,
        in_specs=(
            P("rve", None),
            P("rve"),
            P("rve"),
            P("rve", None),
            P("rve", "gy", "gz", None),
            P("rve", None, None, "gy", "gz", None),
            P(),
        ),
        out_specs=(P("rve", None, None, "gy", "gz", None), P("rve", None)),
        check_vma=False,
    )
```

```python
import functools

import jax
import jax.numpy as jnp
from jax import lax
from jax.experimental import pallas as pl
from jax.experimental.pallas import tpu as pltpu
from jax.sharding import PartitionSpec as P

CAP = 2
SWEEPS = 6
MESH = pl.DeviceIdType.MESH
TANGENT, TARGET, RANK, LISTED = 6, 7, 8, 9


FULL_PRECISION = lax.Precision.HIGHEST
LOWER_BOUND = 0.05
UPPER_BOUND = 1.95


def padded(block, sides, width):
    for axis, dim in sides:
        count = lax.axis_size(axis)
        forward = [(i, i + 1) for i in range(count - 1)]
        forward.append((count - 1, 0))
        backward = [(target, source) for source, target in forward]
        low = lax.ppermute(
            lax.slice_in_dim(block, block.shape[dim] - width, None, axis=dim), axis, forward
        )
        high = lax.ppermute(lax.slice_in_dim(block, 0, width, axis=dim), axis, backward)
        block = jnp.concatenate([low, block, high], axis=dim)
    return block


def chebyshev_weights(sweep_count):
    centre_value = 0.5 * (UPPER_BOUND + LOWER_BOUND)
    half_width = 0.5 * (UPPER_BOUND - LOWER_BOUND)
    ratio_value = centre_value / half_width
    rho_before = 1.0 / ratio_value
    weights = []
    for sweep_index in range(1, sweep_count):
        rho_after = 1.0 / (2.0 * ratio_value - rho_before)
        weights.append((rho_after * rho_before, 2.0 * rho_after / half_width))
        rho_before = rho_after
    return (1.0 / centre_value, weights)


def trim_margin(values_in, margin_have, margin_want, first_dim):
    excess = margin_have - margin_want
    values_in = lax.slice_in_dim(
        values_in, excess, values_in.shape[first_dim] - excess, axis=first_dim
    )
    return lax.slice_in_dim(
        values_in, excess, values_in.shape[first_dim + 1] - excess, axis=first_dim + 1
    )


def apply_stiffness(field_now, moduli, stencil):
    inner_y = field_now.shape[2] - 2
    inner_z = field_now.shape[3] - 2
    centre_mod = moduli[:, 1 : 1 + inner_y, 1 : 1 + inner_z, :]
    running = [None, None, None]
    for shift_y in (-1, 0, 1):
        for shift_z in (-1, 0, 1):
            shifted = field_now[
                :, :, 1 + shift_y : 1 + shift_y + inner_y, 1 + shift_z : 1 + shift_z + inner_z, :
            ]
            shifted_mod = moduli[
                :, 1 + shift_y : 1 + shift_y + inner_y, 1 + shift_z : 1 + shift_z + inner_z, :
            ]
            for shift_x in (-1, 0, 1):
                if shift_x != 0:
                    rolled = jnp.roll(shifted, -shift_x, axis=4)
                    rolled_mod = jnp.roll(shifted_mod, -shift_x, axis=3)
                else:
                    rolled = shifted
                    rolled_mod = shifted_mod
                offset_index = (shift_y + 1) * 9 + (shift_z + 1) * 3 + (shift_x + 1)
                edge_mod = 0.5 * (centre_mod + rolled_mod)
                weighted = [edge_mod * rolled[:, channel_in] for channel_in in range(3)]
                for channel_out in range(3):
                    mixed = stencil[channel_out, 0, offset_index] * weighted[0]
                    mixed = mixed + stencil[channel_out, 1, offset_index] * weighted[1]
                    mixed = mixed + stencil[channel_out, 2, offset_index] * weighted[2]
                    if running[channel_out] is None:
                        running[channel_out] = mixed
                    else:
                        running[channel_out] = running[channel_out] + mixed
    return jnp.stack(running, axis=1)


def body(strain, tangent, yield_list, destination, phase_map, polarization, stencil):
    groups = lax.axis_size("rve")
    rows_here = strain.shape[0]
    yield_count = yield_list.shape[0]
    picker = (jnp.arange(rows_here, dtype=jnp.int32)[None, :] == yield_list[:, None]).astype(
        jnp.float32
    )
    row_strain = jnp.dot(picker, strain, precision=FULL_PRECISION)
    row_tangent = jnp.dot(picker, tangent, precision=FULL_PRECISION)
    target = destination[:, 0]
    positions = jnp.arange(yield_count, dtype=jnp.int32)
    earlier = (target[:, None] == target[None, :]) & (positions[None, :] < positions[:, None])
    rank_in = jnp.sum(earlier.astype(jnp.int32), axis=1)
    group_ids = jnp.arange(groups, dtype=jnp.int32)
    slot_ids = jnp.arange(CAP, dtype=jnp.int32)
    onehot = (
        (target[None, None, :] == group_ids[:, None, None])
        & (rank_in[None, None, :] == slot_ids[None, :, None])
    ).astype(jnp.float32)
    packet = jnp.einsum("gci,ij->gcj", onehot, row_strain, precision=FULL_PRECISION)
    packet_tangent = (
        jnp.einsum("gci,i->gc", onehot, row_tangent, precision=FULL_PRECISION)
        + 1.0
        - jnp.sum(onehot, axis=2)
    )
    parcel = jnp.concatenate([packet, packet_tangent[:, :, None]], axis=2)
    arrived = lax.all_to_all(parcel, "rve", split_axis=0, concat_axis=0, tiled=True)
    slot_strain = arrived[:, :, :6].reshape(groups * CAP, 6)
    slot_tangent = arrived[:, :, 6].reshape(groups * CAP)
    phase_wide = padded(phase_map[0], (("gy", 0), ("gz", 1)), 2)
    moduli_wide = jnp.where(
        phase_wide[None] == 1, slot_tangent[:, None, None, None], jnp.float32(1.0)
    )
    moduli_core = trim_margin(moduli_wide, 2, 0, 1)
    moduli_one = trim_margin(moduli_wide, 2, 1, 1)
    polar_local = polarization[0]
    centre_diag = jnp.diagonal(stencil[:, :, 13])
    body_force = moduli_core[:, None] * jnp.einsum(
        "cjyzx,lj->lcyzx", polar_local, slot_strain, precision=FULL_PRECISION
    )
    inverse_diag = 1.0 / (centre_diag[None, :, None, None, None] * moduli_core[:, None])
    first_weight, weights = chebyshev_weights(SWEEPS)
    update = first_weight * (body_force * inverse_diag)
    field_now = update
    for old_weight, new_weight in weights:
        wrapped = padded(field_now, (("gy", 2), ("gz", 3)), 1)
        residual_now = body_force - apply_stiffness(wrapped, moduli_one, stencil)
        update = old_weight * update + new_weight * (residual_now * inverse_diag)
        field_now = field_now + update
    coupled = jnp.einsum(
        "cjyzx,lcyzx->lj", polar_local, moduli_core[:, None] * field_now, precision=FULL_PRECISION
    )
    partial_value = coupled + slot_strain * jnp.sum(moduli_core, axis=(1, 2, 3))[:, None]
    total_cells = (
        lax.axis_size("gy")
        * lax.axis_size("gz")
        * field_now.shape[2]
        * field_now.shape[3]
        * field_now.shape[4]
    )
    summed = lax.psum(partial_value, ("gy", "gz")) / total_cells
    returned = lax.all_to_all(
        summed.reshape(groups, CAP, 6), "rve", split_axis=0, concat_axis=0, tiled=True
    )
    stress_rows = jnp.einsum("gci,gcj->ij", onehot, returned, precision=FULL_PRECISION)
    return (field_now[None], stress_rows)


def kernel(
    groups, ngy, ngz,
    strain, tangent, yield_list, destination, stencil, phase, polar,
    fields, rows_out,
    tables, slots, phase_all, force_out, force, matrix, spread, field_now, update,
    mod_mid, mod_low, mod_high, mod_inv, sums, partials, totals,
    table_send, table_recv, phase_send, phase_recv, force_send, force_recv,
    field_send, field_recv, part_send, part_recv, total_send, total_recv,
):
    f32, bf16 = jnp.float32, jnp.bfloat16
    channels, strains = polar.shape[1], polar.shape[2]
    y_here, z_here, nx = polar.shape[3:]
    ny, nz = y_here * ngy, z_here * ngz
    wide = channels * nz
    slot_rows = 3 * wide
    depth = 3 * slot_rows
    listed = yield_list.shape[0]
    loads = groups * CAP
    my_r, my_y, my_z = lax.axis_index("rve"), lax.axis_index("gy"), lax.axis_index("gz")
    my_load = my_y * ngz + my_z

    def turned(base, step, count):
        return lax.rem(base + step + count, count)

    mates = [(dy, dz) for dy in list(range(1, ngy)) + [0] for dz in list(range(1, ngz)) + [0]]
    others = [mate for mate in mates if mate != (0, 0)]

    def mate_id(dy, dz):
        return {"gy": turned(my_y, dy, ngy), "gz": turned(my_z, dz, ngz)}

    def block(dy, dz):
        y_at = turned(my_y, dy, ngy) * y_here
        z_at = pl.multiple_of(turned(my_z, dz, ngz) * z_here, 8)
        return pl.ds(y_at, y_here), pl.ds(z_at, z_here)

    barrier = pltpu.get_barrier_semaphore()
    for dy, dz in others:
        pl.semaphore_signal(barrier, inc=1, device_id=mate_id(dy, dz), device_id_type=MESH)
    for step in range(1, groups):
        pl.semaphore_signal(
            barrier, inc=1, device_id={"rve": turned(my_r, step, groups)}, device_id_type=MESH
        )

    row_ids = lax.broadcasted_iota(jnp.int32, (8, 128), 0)
    lane_ids = lax.broadcasted_iota(jnp.int32, (8, 128), 1)
    table = jnp.zeros((8, 128), f32)
    for i in range(listed):
        point, target = yield_list[i], destination[i, 0]
        rank = jnp.int32(0)
        for k in range(i):
            rank = rank + jnp.where(destination[k, 0] == target, 1, 0)
        values = [strain[point, j] for j in range(strains)]
        values += [tangent[point], target.astype(f32), rank.astype(f32), jnp.float32(1.0)]
        for j, value in enumerate(values):
            table = jnp.where((row_ids == i) & (lane_ids == j), value, table)
    tables[my_r] = table

    pl.semaphore_wait(barrier, len(others) + groups - 1)

    def table_copy(step, owner):
        return pltpu.make_async_remote_copy(
            src_ref=tables.at[my_r], dst_ref=tables.at[owner],
            send_sem=table_send.at[step], recv_sem=table_recv.at[step],
            device_id={"rve": turned(my_r, step, groups)}, device_id_type=MESH,
        )

    def phase_copy(index, dy, dz):
        y_at, z_at = block(dy, dz)
        to_y, to_z = others[index]
        return pltpu.make_async_remote_copy(
            src_ref=phase.at[0], dst_ref=phase_all.at[y_at, z_at],
            send_sem=phase_send.at[index], recv_sem=phase_recv.at[index],
            device_id=mate_id(to_y, to_z), device_id_type=MESH,
        )

    for step in range(1, groups):
        table_copy(step, my_r).start()
    for index in range(len(others)):
        phase_copy(index, 0, 0).start()
    own_y, own_z = block(0, 0)
    phase_all[own_y, own_z, :] = phase[0]

    for step in range(1, groups):
        table_copy(step, turned(my_r, -step, groups)).wait_recv()
    for source in range(groups):
        heard = tables[source]
        named = (heard[:, TARGET : TARGET + 1] == my_r.astype(f32)) & (
            heard[:, LISTED : LISTED + 1] == 1.0
        )
        for rank in range(CAP):
            chosen = named & (heard[:, RANK : RANK + 1] == float(rank))
            line = jnp.sum(jnp.where(chosen, heard, 0.0), axis=0, keepdims=True)
            missing = 1.0 - line[:, LISTED : LISTED + 1]
            line = line + jnp.where(lane_ids[:1] == TANGENT, missing, 0.0)
            at = source * CAP + rank
            slots[at : at + 1, :] = line

    def slot_value(load, index):
        return jnp.broadcast_to(slots[pl.ds(load, 1), :][:, index : index + 1], (8, 128))

    def force_copy(index, dy, dz):
        y_at, z_at = block(dy, dz)
        return pltpu.make_async_remote_copy(
            src_ref=force_out.at[index], dst_ref=force.at[:, y_at, z_at],
            send_sem=force_send.at[index], recv_sem=force_recv.at[index],
            device_id=mate_id(*others[index]), device_id_type=MESH,
        )

    for index, (dy, dz) in enumerate(mates):
        load = turned(my_y, dy, ngy) * ngz + turned(my_z, dz, ngz)
        strain_of = [slot_value(load, j) for j in range(strains)]
        for c in range(channels):
            for y in range(y_here):
                value = polar[0, c, 0, y] * strain_of[0]
                for j in range(1, strains):
                    value = value + polar[0, c, j, y] * strain_of[j]
                if (dy, dz) == (0, 0):
                    force[c, my_y * y_here + y, own_z, :] = value
                else:
                    force_out[index, c, y] = value
        if (dy, dz) != (0, 0):
            force_copy(index, 0, 0).start()

    column = lax.broadcasted_iota(jnp.int32, (1, depth), 1)
    column_y = column // slot_rows
    column_kind = lax.rem(column, slot_rows) // wide
    column_d = lax.rem(column, wide) // nz
    picks = [[(column_y == dy) & (column_d == d) for d in range(channels)] for dy in range(3)]
    z_row = lax.broadcasted_iota(jnp.int32, (nz, depth), 0)
    z_column = lax.rem(lax.broadcasted_iota(jnp.int32, (nz, depth), 1), nz)
    bands = [z_column == lax.rem(z_row + dz - 1 + nz, nz) for dz in range(3)]
    is_low = jnp.broadcast_to(column_kind, (nz, depth)) == 1
    for dx in range(3):
        for c in range(channels):
            values = jnp.zeros((nz, depth), f32)
            for dz in range(3):
                line = jnp.zeros((1, depth), f32)
                for dy in range(3):
                    for d in range(channels):
                        line = jnp.where(
                            picks[dy][d], 0.5 * stencil[c, d, dy * 9 + dz * 3 + dx], line
                        )
                values = values + jnp.where(bands[dz], line, 0.0)
            high = values.astype(bf16).astype(f32)
            low = values - high
            at = (dx * channels + c) * nz
            matrix[at : at + nz, :] = jnp.where(is_low, low, high).astype(bf16)

    for index, (dy, dz) in enumerate(others):
        phase_copy(index, -dy, -dz).wait_recv()
    tangent_row = slots[pl.ds(my_load, 1), :][:, TANGENT : TANGENT + 1]
    my_tangent = jnp.broadcast_to(tangent_row, (nz, nx))
    inverse_tangent = 1.0 / my_tangent
    for y in range(ny):
        second = phase_all[y] == 1
        mod = jnp.where(second, my_tangent, 1.0)
        mod_mid[y] = mod
        mod_low[y] = pltpu.roll(mod, nx - 1, 1)
        mod_high[y] = pltpu.roll(mod, 1, 1)
        mod_inv[y] = jnp.where(second, inverse_tangent, 1.0)
    ones = jnp.ones((nz, nx), f32)
    inverse_centre = [1.0 / (ones * stencil[c, c, 13]) for c in range(channels)]

    def put(buffer, y, c, value):
        both = jnp.concatenate([value, value * mod_mid[y]], axis=1)
        high = both.astype(bf16)
        low = (both - high.astype(f32)).astype(bf16)
        at = pl.multiple_of((y + 1) * slot_rows + c * nz, 16)
        spread[buffer, pl.ds(at, nz), :] = high
        spread[buffer, pl.ds(at + wide, nz), :] = high
        spread[buffer, pl.ds(at + 2 * wide, nz), :] = low

    def wrap(buffer):
        spread[buffer, 0:slot_rows, :] = spread[buffer, ny * slot_rows : (ny + 1) * slot_rows, :]
        spread[buffer, (ny + 1) * slot_rows : (ny + 2) * slot_rows, :] = spread[
            buffer, slot_rows : 2 * slot_rows, :
        ]

    for index, (dy, dz) in enumerate(others):
        force_copy(index, -dy, -dz).wait_recv()
    first_weight, weights = chebyshev_weights(SWEEPS)
    for y in range(ny):
        for c in range(channels):
            value = first_weight * (force[c, y] * inverse_centre[c])
            update[c, y] = value
            field_now[c, y] = value
            put(0, y, c, value)
    wrap(0)

    def sweep_row(buffer, y, old_weight, new_weight, last):
        at = y * slot_rows if isinstance(y, int) else pl.multiple_of(y * slot_rows, 16)
        product = jnp.dot(
            matrix[...], spread[buffer, pl.ds(at, depth), :], preferred_element_type=f32
        )
        for c in range(channels):
            parts = []
            for dx, mod in enumerate((mod_low, mod_mid, mod_high)):
                row = (dx * channels + c) * nz
                parts.append(
                    mod[y] * product[row : row + nz, :nx] + product[row : row + nz, nx:]
                )
            stiff = parts[1] + pltpu.roll(parts[0], 1, 1) + pltpu.roll(parts[2], nx - 1, 1)
            residual = (force[c, y] - stiff * mod_inv[y]) * inverse_centre[c]
            step = old_weight * update[c, y] + new_weight * residual
            value = field_now[c, y] + step
            field_now[c, y] = value
            if not last:
                update[c, y] = step
                put(1 - buffer, y, c, value)

    def sweep(k, carry):
        old_weight, new_weight = jnp.float32(weights[0][0]), jnp.float32(weights[0][1])
        for position in range(1, len(weights) - 1):
            old_weight = jnp.where(k == position, weights[position][0], old_weight)
            new_weight = jnp.where(k == position, weights[position][1], new_weight)
        buffer = lax.rem(k, 2)
        for y in range(ny):
            sweep_row(buffer, y, old_weight, new_weight, False)
        wrap(1 - buffer)
        return carry

    lax.fori_loop(0, len(weights) - 1, sweep, 0)

    def field_copy(dy, dz, y, load):
        to_y, to_z = turned(my_y, dy, ngy), turned(my_z, dz, ngz)
        z_at = pl.ds(pl.multiple_of(to_z * z_here, 8), z_here)
        return pltpu.make_async_remote_copy(
            src_ref=field_now.at[:, to_y * y_here + y, z_at],
            dst_ref=fields.at[0, load, :, y],
            send_sem=field_send.at[dy, dz, y], recv_sem=field_recv.at[dy, dz, y],
            device_id={"gy": to_y, "gz": to_z}, device_id_type=MESH,
        )

    final_buffer = (len(weights) - 1) % 2
    for dy in list(range(1, ngy)) + [0]:
        for y in range(y_here):
            row = turned(my_y, dy, ngy) * y_here + y
            sweep_row(final_buffer, row, weights[-1][0], weights[-1][1], True)
            for dz in list(range(1, ngz)) + [0]:
                if (dy, dz) != (0, 0):
                    field_copy(dy, dz, y, my_load).start()
                else:
                    for c in range(channels):
                        fields[0, my_load, c, y] = field_now[c, row, own_z, :]

    seconds = [phase[0, y] == 1 for y in range(y_here)]
    for dy, dz in mates:
        load = turned(my_y, -dy, ngy) * ngz + turned(my_z, -dz, ngz)
        if (dy, dz) != (0, 0):
            for y in range(y_here):
                field_copy(dy, dz, y, load).wait_recv()
        slope = slot_value(load, TANGENT)
        totals_of = [jnp.zeros((8, 128), f32) for _ in range(strains)]
        for y in range(y_here):
            mod = jnp.where(seconds[y], slope, 1.0)
            for c in range(channels):
                flux = mod * fields[0, load, c, y]
                for j in range(strains):
                    totals_of[j] = totals_of[j] + polar[0, c, j, y] * flux
        for j in range(strains):
            sums[j, pl.ds(load, 1), :] = jnp.sum(totals_of[j], axis=0, keepdims=True)
    ones_here = jnp.zeros((8, 128), f32)
    for y in range(y_here):
        ones_here = ones_here + jnp.where(seconds[y], 1.0, 0.0)
    second_count = jnp.sum(jnp.sum(ones_here, axis=0, keepdims=True), axis=1, keepdims=True)
    slot_table = slots[...]
    mod_sum = second_count * slot_table[:, TANGENT : TANGENT + 1] + (
        float(y_here * z_here * nx) - second_count
    )
    share = jnp.where(lane_ids < strains, slot_table * mod_sum, 0.0)
    for j in range(strains):
        share = share + jnp.where(
            lane_ids == j, jnp.sum(sums[j], axis=1, keepdims=True), 0.0
        )
    partials[len(others)] = share * (1.0 / (ny * nz * nx))

    def part_copy(index):
        return pltpu.make_async_remote_copy(
            src_ref=partials.at[len(others)], dst_ref=partials.at[index],
            send_sem=part_send.at[index], recv_sem=part_recv.at[index],
            device_id=mate_id(*others[index]), device_id_type=MESH,
        )

    for index in range(len(others)):
        part_copy(index).start()
    for index in range(len(others)):
        part_copy(index).wait_recv()
    total = partials[0]
    for index in range(1, len(mates)):
        total = total + partials[index]
    totals[my_r] = total

    def total_copy(step, owner):
        return pltpu.make_async_remote_copy(
            src_ref=totals.at[my_r], dst_ref=totals.at[owner],
            send_sem=total_send.at[step], recv_sem=total_recv.at[step],
            device_id={"rve": turned(my_r, step, groups)}, device_id_type=MESH,
        )

    for step in range(1, groups):
        total_copy(step, my_r).start()
    for step in range(1, groups):
        total_copy(step, turned(my_r, -step, groups)).wait_recv()
    mine = tables[my_r]
    answer = jnp.zeros((8, 128), f32)
    for group in range(groups):
        for rank in range(CAP):
            chosen = (mine[:, TARGET : TARGET + 1] == float(group)) & (
                mine[:, RANK : RANK + 1] == float(rank)
            )
            line = totals[group, pl.ds(my_r * CAP + rank, 1), :]
            answer = answer + jnp.where(chosen, line, 0.0)
    rows_out[...] = answer[:listed, :strains]

    for step in range(1, groups):
        table_copy(step, my_r).wait_send()
        total_copy(step, my_r).wait_send()
    for index, (dy, dz) in enumerate(others):
        phase_copy(index, 0, 0).wait_send()
        force_copy(index, 0, 0).wait_send()
        part_copy(index).wait_send()
        for y in range(y_here):
            field_copy(dy, dz, y, my_load).wait_send()


def fused_body(strain, tangent, yield_list, destination, phase_map, polarization, stencil):
    groups, ngy, ngz = (lax.axis_size(name) for name in ("rve", "gy", "gz"))
    channels = polarization.shape[1]
    strains = polarization.shape[2]
    y_here, z_here, nx = polarization.shape[3:]
    ny, nz = y_here * ngy, z_here * ngz
    loads = groups * CAP
    count = ngy * ngz
    f32 = jnp.float32
    slot_rows = 3 * channels * nz
    vmem = pl.BlockSpec(memory_space=pltpu.VMEM)
    smem = pl.BlockSpec(memory_space=pltpu.SMEM)
    cell = pltpu.VMEM((ny, nz, nx), f32)
    vector = pltpu.VMEM((channels, ny, nz, nx), f32)

    def dma(*shape):
        return pltpu.SemaphoreType.DMA(shape)

    return pl.pallas_call(
        functools.partial(kernel, groups, ngy, ngz),
        out_shape=(
            jax.ShapeDtypeStruct((1, loads, channels, y_here, z_here, nx), f32),
            jax.ShapeDtypeStruct((yield_list.shape[0], strains), f32),
        ),
        in_specs=[smem, smem, smem, smem, smem, vmem, vmem],
        out_specs=(vmem, vmem),
        scratch_shapes=[
            pltpu.VMEM((groups, 8, 128), f32),
            pltpu.VMEM((loads, 128), f32),
            pltpu.VMEM((ny, nz, nx), jnp.int32),
            pltpu.VMEM((count, channels, y_here, z_here, nx), f32),
            vector,
            pltpu.VMEM((3 * channels * nz, 3 * slot_rows), jnp.bfloat16),
            pltpu.VMEM((2, (ny + 2) * slot_rows, 2 * nx), jnp.bfloat16),
            vector,
            vector,
            cell, cell, cell, cell,
            pltpu.VMEM((strains, loads, 128), f32),
            pltpu.VMEM((count, 8, 128), f32),
            pltpu.VMEM((groups, 8, 128), f32),
            dma(groups), dma(groups), dma(count), dma(count), dma(count), dma(count),
            dma(ngy, ngz, y_here), dma(ngy, ngz, y_here),
            dma(count), dma(count), dma(groups), dma(groups),
        ],
        compiler_params=pltpu.CompilerParams(
            collective_id=0, has_side_effects=True, vmem_limit_bytes=40 * 1024 * 1024
        ),
    )(strain, tangent, yield_list, destination, stencil, phase_map, polarization)


def body_for(mesh):
    def chosen(*arguments):
        strain, _, yield_list, _, phase_map, _, _ = arguments
        loads = lax.axis_size("rve") * CAP
        one_load_each = lax.axis_size("gy") * lax.axis_size("gz") == loads
        tiled = phase_map.shape[2] == 8 and phase_map.shape[3] == 128 and loads == 8
        if one_load_each and tiled and yield_list.shape[0] <= 8:
            return fused_body(*arguments)
        return body(*arguments)

    return chosen


def solution(mesh):
    return jax.shard_map(
        body_for(mesh),
        mesh=mesh,
        in_specs=(
            P("rve", None),
            P("rve"),
            P("rve"),
            P("rve", None),
            P("rve", "gy", "gz", None),
            P("rve", None, None, "gy", "gz", None),
            P(),
        ),
        out_specs=(P("rve", None, None, "gy", "gz", None), P("rve", None)),
        check_vma=False,
    )
```

```python
import functools

import jax
import jax.numpy as jnp
from jax import lax
from jax.experimental import pallas as pl
from jax.experimental.pallas import tpu as pltpu
from jax.sharding import PartitionSpec as P

CAP = 2
SWEEPS = 6
MESH = pl.DeviceIdType.MESH
TANGENT, TARGET, RANK, LISTED = 6, 7, 8, 9


FULL_PRECISION = lax.Precision.HIGHEST
LOWER_BOUND = 0.05
UPPER_BOUND = 1.95


def padded(block, sides, width):
    for axis, dim in sides:
        count = lax.axis_size(axis)
        forward = [(i, i + 1) for i in range(count - 1)]
        forward.append((count - 1, 0))
        backward = [(target, source) for source, target in forward]
        low = lax.ppermute(
            lax.slice_in_dim(block, block.shape[dim] - width, None, axis=dim), axis, forward
        )
        high = lax.ppermute(lax.slice_in_dim(block, 0, width, axis=dim), axis, backward)
        block = jnp.concatenate([low, block, high], axis=dim)
    return block


def chebyshev_weights(sweep_count):
    centre_value = 0.5 * (UPPER_BOUND + LOWER_BOUND)
    half_width = 0.5 * (UPPER_BOUND - LOWER_BOUND)
    ratio_value = centre_value / half_width
    rho_before = 1.0 / ratio_value
    weights = []
    for sweep_index in range(1, sweep_count):
        rho_after = 1.0 / (2.0 * ratio_value - rho_before)
        weights.append((rho_after * rho_before, 2.0 * rho_after / half_width))
        rho_before = rho_after
    return (1.0 / centre_value, weights)


def trim_margin(values_in, margin_have, margin_want, first_dim):
    excess = margin_have - margin_want
    values_in = lax.slice_in_dim(
        values_in, excess, values_in.shape[first_dim] - excess, axis=first_dim
    )
    return lax.slice_in_dim(
        values_in, excess, values_in.shape[first_dim + 1] - excess, axis=first_dim + 1
    )


def apply_stiffness(field_now, moduli, stencil):
    inner_y = field_now.shape[2] - 2
    inner_z = field_now.shape[3] - 2
    centre_mod = moduli[:, 1 : 1 + inner_y, 1 : 1 + inner_z, :]
    running = [None, None, None]
    for shift_y in (-1, 0, 1):
        for shift_z in (-1, 0, 1):
            shifted = field_now[
                :, :, 1 + shift_y : 1 + shift_y + inner_y, 1 + shift_z : 1 + shift_z + inner_z, :
            ]
            shifted_mod = moduli[
                :, 1 + shift_y : 1 + shift_y + inner_y, 1 + shift_z : 1 + shift_z + inner_z, :
            ]
            for shift_x in (-1, 0, 1):
                if shift_x != 0:
                    rolled = jnp.roll(shifted, -shift_x, axis=4)
                    rolled_mod = jnp.roll(shifted_mod, -shift_x, axis=3)
                else:
                    rolled = shifted
                    rolled_mod = shifted_mod
                offset_index = (shift_y + 1) * 9 + (shift_z + 1) * 3 + (shift_x + 1)
                edge_mod = 0.5 * (centre_mod + rolled_mod)
                weighted = [edge_mod * rolled[:, channel_in] for channel_in in range(3)]
                for channel_out in range(3):
                    mixed = stencil[channel_out, 0, offset_index] * weighted[0]
                    mixed = mixed + stencil[channel_out, 1, offset_index] * weighted[1]
                    mixed = mixed + stencil[channel_out, 2, offset_index] * weighted[2]
                    if running[channel_out] is None:
                        running[channel_out] = mixed
                    else:
                        running[channel_out] = running[channel_out] + mixed
    return jnp.stack(running, axis=1)


def body(strain, tangent, yield_list, destination, phase_map, polarization, stencil):
    groups = lax.axis_size("rve")
    rows_here = strain.shape[0]
    yield_count = yield_list.shape[0]
    picker = (jnp.arange(rows_here, dtype=jnp.int32)[None, :] == yield_list[:, None]).astype(
        jnp.float32
    )
    row_strain = jnp.dot(picker, strain, precision=FULL_PRECISION)
    row_tangent = jnp.dot(picker, tangent, precision=FULL_PRECISION)
    target = destination[:, 0]
    positions = jnp.arange(yield_count, dtype=jnp.int32)
    earlier = (target[:, None] == target[None, :]) & (positions[None, :] < positions[:, None])
    rank_in = jnp.sum(earlier.astype(jnp.int32), axis=1)
    group_ids = jnp.arange(groups, dtype=jnp.int32)
    slot_ids = jnp.arange(CAP, dtype=jnp.int32)
    onehot = (
        (target[None, None, :] == group_ids[:, None, None])
        & (rank_in[None, None, :] == slot_ids[None, :, None])
    ).astype(jnp.float32)
    packet = jnp.einsum("gci,ij->gcj", onehot, row_strain, precision=FULL_PRECISION)
    packet_tangent = (
        jnp.einsum("gci,i->gc", onehot, row_tangent, precision=FULL_PRECISION)
        + 1.0
        - jnp.sum(onehot, axis=2)
    )
    parcel = jnp.concatenate([packet, packet_tangent[:, :, None]], axis=2)
    arrived = lax.all_to_all(parcel, "rve", split_axis=0, concat_axis=0, tiled=True)
    slot_strain = arrived[:, :, :6].reshape(groups * CAP, 6)
    slot_tangent = arrived[:, :, 6].reshape(groups * CAP)
    phase_wide = padded(phase_map[0], (("gy", 0), ("gz", 1)), 2)
    moduli_wide = jnp.where(
        phase_wide[None] == 1, slot_tangent[:, None, None, None], jnp.float32(1.0)
    )
    moduli_core = trim_margin(moduli_wide, 2, 0, 1)
    moduli_one = trim_margin(moduli_wide, 2, 1, 1)
    polar_local = polarization[0]
    centre_diag = jnp.diagonal(stencil[:, :, 13])
    body_force = moduli_core[:, None] * jnp.einsum(
        "cjyzx,lj->lcyzx", polar_local, slot_strain, precision=FULL_PRECISION
    )
    inverse_diag = 1.0 / (centre_diag[None, :, None, None, None] * moduli_core[:, None])
    first_weight, weights = chebyshev_weights(SWEEPS)
    update = first_weight * (body_force * inverse_diag)
    field_now = update
    for old_weight, new_weight in weights:
        wrapped = padded(field_now, (("gy", 2), ("gz", 3)), 1)
        residual_now = body_force - apply_stiffness(wrapped, moduli_one, stencil)
        update = old_weight * update + new_weight * (residual_now * inverse_diag)
        field_now = field_now + update
    coupled = jnp.einsum(
        "cjyzx,lcyzx->lj", polar_local, moduli_core[:, None] * field_now, precision=FULL_PRECISION
    )
    partial_value = coupled + slot_strain * jnp.sum(moduli_core, axis=(1, 2, 3))[:, None]
    total_cells = (
        lax.axis_size("gy")
        * lax.axis_size("gz")
        * field_now.shape[2]
        * field_now.shape[3]
        * field_now.shape[4]
    )
    summed = lax.psum(partial_value, ("gy", "gz")) / total_cells
    returned = lax.all_to_all(
        summed.reshape(groups, CAP, 6), "rve", split_axis=0, concat_axis=0, tiled=True
    )
    stress_rows = jnp.einsum("gci,gcj->ij", onehot, returned, precision=FULL_PRECISION)
    return (field_now[None], stress_rows)


def kernel(
    groups, ngy, ngz,
    strain, tangent, yield_list, destination, stencil, phase, polar,
    fields, rows_out,
    tables, slots, phase_all, force_out, force, matrix, spread, field_now, update,
    mod_mid, mod_low, mod_high, mod_inv, sums, partials, totals,
    table_send, table_recv, phase_send, phase_recv, force_send, force_recv,
    field_send, field_recv, part_send, part_recv, total_send, total_recv,
):
    f32, bf16 = jnp.float32, jnp.bfloat16
    channels, strains = polar.shape[1], polar.shape[2]
    y_here, z_here, nx = polar.shape[3:]
    ny, nz = y_here * ngy, z_here * ngz
    wide = channels * nz
    slot_rows = 3 * wide
    depth = 3 * slot_rows
    listed = yield_list.shape[0]
    loads = groups * CAP
    my_r, my_y, my_z = lax.axis_index("rve"), lax.axis_index("gy"), lax.axis_index("gz")
    my_load = my_y * ngz + my_z

    def turned(base, step, count):
        return lax.rem(base + step + count, count)

    mates = [(dy, dz) for dy in list(range(1, ngy)) + [0] for dz in list(range(1, ngz)) + [0]]
    others = [mate for mate in mates if mate != (0, 0)]

    def mate_id(dy, dz):
        return {"gy": turned(my_y, dy, ngy), "gz": turned(my_z, dz, ngz)}

    def block(dy, dz):
        y_at = turned(my_y, dy, ngy) * y_here
        z_at = pl.multiple_of(turned(my_z, dz, ngz) * z_here, 8)
        return pl.ds(y_at, y_here), pl.ds(z_at, z_here)

    barrier = pltpu.get_barrier_semaphore()
    for dy, dz in others:
        pl.semaphore_signal(barrier, inc=1, device_id=mate_id(dy, dz), device_id_type=MESH)
    for step in range(1, groups):
        pl.semaphore_signal(
            barrier, inc=1, device_id={"rve": turned(my_r, step, groups)}, device_id_type=MESH
        )

    row_ids = lax.broadcasted_iota(jnp.int32, (8, 128), 0)
    lane_ids = lax.broadcasted_iota(jnp.int32, (8, 128), 1)
    table = jnp.zeros((8, 128), f32)
    for i in range(listed):
        point, target = yield_list[i], destination[i, 0]
        rank = jnp.int32(0)
        for k in range(i):
            rank = rank + jnp.where(destination[k, 0] == target, 1, 0)
        values = [strain[point, j] for j in range(strains)]
        values += [tangent[point], target.astype(f32), rank.astype(f32), jnp.float32(1.0)]
        for j, value in enumerate(values):
            table = jnp.where((row_ids == i) & (lane_ids == j), value, table)
    tables[my_r] = table

    pl.semaphore_wait(barrier, len(others) + groups - 1)

    def table_copy(step, owner):
        return pltpu.make_async_remote_copy(
            src_ref=tables.at[my_r], dst_ref=tables.at[owner],
            send_sem=table_send.at[step], recv_sem=table_recv.at[step],
            device_id={"rve": turned(my_r, step, groups)}, device_id_type=MESH,
        )

    def phase_copy(index, dy, dz):
        y_at, z_at = block(dy, dz)
        to_y, to_z = others[index]
        return pltpu.make_async_remote_copy(
            src_ref=phase.at[0], dst_ref=phase_all.at[y_at, z_at],
            send_sem=phase_send.at[index], recv_sem=phase_recv.at[index],
            device_id=mate_id(to_y, to_z), device_id_type=MESH,
        )

    for step in range(1, groups):
        table_copy(step, my_r).start()
    for index in range(len(others)):
        phase_copy(index, 0, 0).start()
    own_y, own_z = block(0, 0)
    phase_all[own_y, own_z, :] = phase[0]

    for step in range(1, groups):
        table_copy(step, turned(my_r, -step, groups)).wait_recv()
    for source in range(groups):
        heard = tables[source]
        named = (heard[:, TARGET : TARGET + 1] == my_r.astype(f32)) & (
            heard[:, LISTED : LISTED + 1] == 1.0
        )
        for rank in range(CAP):
            chosen = named & (heard[:, RANK : RANK + 1] == float(rank))
            line = jnp.sum(jnp.where(chosen, heard, 0.0), axis=0, keepdims=True)
            missing = 1.0 - line[:, LISTED : LISTED + 1]
            line = line + jnp.where(lane_ids[:1] == TANGENT, missing, 0.0)
            at = source * CAP + rank
            slots[at : at + 1, :] = line

    def slot_value(load, index):
        return jnp.broadcast_to(slots[pl.ds(load, 1), :][:, index : index + 1], (8, 128))

    def force_copy(index, dy, dz):
        y_at, z_at = block(dy, dz)
        return pltpu.make_async_remote_copy(
            src_ref=force_out.at[index], dst_ref=force.at[:, y_at, z_at],
            send_sem=force_send.at[index], recv_sem=force_recv.at[index],
            device_id=mate_id(*others[index]), device_id_type=MESH,
        )

    for index, (dy, dz) in enumerate(mates):
        load = turned(my_y, dy, ngy) * ngz + turned(my_z, dz, ngz)
        strain_of = [slot_value(load, j) for j in range(strains)]
        for c in range(channels):
            for y in range(y_here):
                value = polar[0, c, 0, y] * strain_of[0]
                for j in range(1, strains):
                    value = value + polar[0, c, j, y] * strain_of[j]
                if (dy, dz) == (0, 0):
                    force[c, my_y * y_here + y, own_z, :] = value
                else:
                    force_out[index, c, y] = value
        if (dy, dz) != (0, 0):
            force_copy(index, 0, 0).start()

    column = lax.broadcasted_iota(jnp.int32, (1, depth), 1)
    column_y = column // slot_rows
    column_kind = lax.rem(column, slot_rows) // wide
    column_d = lax.rem(column, wide) // nz
    picks = [[(column_y == dy) & (column_d == d) for d in range(channels)] for dy in range(3)]
    z_row = lax.broadcasted_iota(jnp.int32, (nz, depth), 0)
    z_column = lax.rem(lax.broadcasted_iota(jnp.int32, (nz, depth), 1), nz)
    bands = [z_column == lax.rem(z_row + dz - 1 + nz, nz) for dz in range(3)]
    is_low = jnp.broadcast_to(column_kind, (nz, depth)) == 1
    for dx in range(3):
        for c in range(channels):
            values = jnp.zeros((nz, depth), f32)
            for dz in range(3):
                line = jnp.zeros((1, depth), f32)
                for dy in range(3):
                    for d in range(channels):
                        line = jnp.where(
                            picks[dy][d], 0.5 * stencil[c, d, dy * 9 + dz * 3 + dx], line
                        )
                values = values + jnp.where(bands[dz], line, 0.0)
            high = values.astype(bf16).astype(f32)
            low = values - high
            at = (dx * channels + c) * nz
            matrix[at : at + nz, :] = jnp.where(is_low, low, high).astype(bf16)

    for index, (dy, dz) in enumerate(others):
        phase_copy(index, -dy, -dz).wait_recv()
    tangent_row = slots[pl.ds(my_load, 1), :][:, TANGENT : TANGENT + 1]
    my_tangent = jnp.broadcast_to(tangent_row, (nz, nx))
    inverse_tangent = 1.0 / my_tangent
    for y in range(ny):
        second = phase_all[y] == 1
        mod = jnp.where(second, my_tangent, 1.0)
        mod_mid[y] = mod
        mod_low[y] = pltpu.roll(mod, nx - 1, 1)
        mod_high[y] = pltpu.roll(mod, 1, 1)
        mod_inv[y] = jnp.where(second, inverse_tangent, 1.0)
    ones = jnp.ones((nz, nx), f32)
    inverse_centre = [1.0 / (ones * stencil[c, c, 13]) for c in range(channels)]

    def put(buffer, y, c, value):
        both = jnp.concatenate([value, value * mod_mid[y]], axis=1)
        high = both.astype(bf16)
        low = (both - high.astype(f32)).astype(bf16)
        at = pl.multiple_of((y + 1) * slot_rows + c * nz, 16)
        spread[buffer, pl.ds(at, nz), :] = high
        spread[buffer, pl.ds(at + wide, nz), :] = high
        spread[buffer, pl.ds(at + 2 * wide, nz), :] = low

    def wrap(buffer):
        spread[buffer, 0:slot_rows, :] = spread[buffer, ny * slot_rows : (ny + 1) * slot_rows, :]
        spread[buffer, (ny + 1) * slot_rows : (ny + 2) * slot_rows, :] = spread[
            buffer, slot_rows : 2 * slot_rows, :
        ]

    for index, (dy, dz) in enumerate(others):
        force_copy(index, -dy, -dz).wait_recv()
    first_weight, weights = chebyshev_weights(SWEEPS)
    for y in range(ny):
        for c in range(channels):
            value = first_weight * (force[c, y] * inverse_centre[c])
            update[c, y] = value
            field_now[c, y] = value
            put(0, y, c, value)
    wrap(0)

    def sweep_row(buffer, y, old_weight, new_weight, last):
        at = y * slot_rows if isinstance(y, int) else pl.multiple_of(y * slot_rows, 16)
        product = jnp.dot(
            matrix[...], spread[buffer, pl.ds(at, depth), :], preferred_element_type=f32
        )
        for c in range(channels):
            parts = []
            for dx, mod in enumerate((mod_low, mod_mid, mod_high)):
                row = (dx * channels + c) * nz
                parts.append(
                    mod[y] * product[row : row + nz, :nx] + product[row : row + nz, nx:]
                )
            stiff = parts[1] + pltpu.roll(parts[0], 1, 1) + pltpu.roll(parts[2], nx - 1, 1)
            residual = (force[c, y] - stiff * mod_inv[y]) * inverse_centre[c]
            step = old_weight * update[c, y] + new_weight * residual
            value = field_now[c, y] + step
            field_now[c, y] = value
            if not last:
                update[c, y] = step
                put(1 - buffer, y, c, value)

    def sweep_pair(pair, carry):
        for buffer in range(2):
            k = pair * 2 + buffer
            old_weight, new_weight = jnp.float32(weights[0][0]), jnp.float32(weights[0][1])
            for position in range(1, len(weights) - 1):
                old_weight = jnp.where(k == position, weights[position][0], old_weight)
                new_weight = jnp.where(k == position, weights[position][1], new_weight)
            for y in range(ny):
                sweep_row(buffer, y, old_weight, new_weight, False)
            wrap(1 - buffer)
        return carry

    assert len(weights) % 2 == 1
    lax.fori_loop(0, (len(weights) - 1) // 2, sweep_pair, 0)

    def field_copy(dy, dz, y, load):
        to_y, to_z = turned(my_y, dy, ngy), turned(my_z, dz, ngz)
        z_at = pl.ds(pl.multiple_of(to_z * z_here, 8), z_here)
        return pltpu.make_async_remote_copy(
            src_ref=field_now.at[:, to_y * y_here + y, z_at],
            dst_ref=fields.at[0, load, :, y],
            send_sem=field_send.at[dy, dz, y], recv_sem=field_recv.at[dy, dz, y],
            device_id={"gy": to_y, "gz": to_z}, device_id_type=MESH,
        )

    final_buffer = (len(weights) - 1) % 2
    for dy in list(range(1, ngy)) + [0]:
        for y in range(y_here):
            row = turned(my_y, dy, ngy) * y_here + y
            sweep_row(final_buffer, row, weights[-1][0], weights[-1][1], True)
            for dz in list(range(1, ngz)) + [0]:
                if (dy, dz) != (0, 0):
                    field_copy(dy, dz, y, my_load).start()
                else:
                    for c in range(channels):
                        fields[0, my_load, c, y] = field_now[c, row, own_z, :]

    seconds = [phase[0, y] == 1 for y in range(y_here)]
    for dy, dz in mates:
        load = turned(my_y, -dy, ngy) * ngz + turned(my_z, -dz, ngz)
        if (dy, dz) != (0, 0):
            for y in range(y_here):
                field_copy(dy, dz, y, load).wait_recv()
        slope = slot_value(load, TANGENT)
        totals_of = [jnp.zeros((8, 128), f32) for _ in range(strains)]
        for y in range(y_here):
            mod = jnp.where(seconds[y], slope, 1.0)
            for c in range(channels):
                flux = mod * fields[0, load, c, y]
                for j in range(strains):
                    totals_of[j] = totals_of[j] + polar[0, c, j, y] * flux
        for j in range(strains):
            sums[j, pl.ds(load, 1), :] = jnp.sum(totals_of[j], axis=0, keepdims=True)
    ones_here = jnp.zeros((8, 128), f32)
    for y in range(y_here):
        ones_here = ones_here + jnp.where(seconds[y], 1.0, 0.0)
    second_count = jnp.sum(jnp.sum(ones_here, axis=0, keepdims=True), axis=1, keepdims=True)
    slot_table = slots[...]
    mod_sum = second_count * slot_table[:, TANGENT : TANGENT + 1] + (
        float(y_here * z_here * nx) - second_count
    )
    share = jnp.where(lane_ids < strains, slot_table * mod_sum, 0.0)
    for j in range(strains):
        share = share + jnp.where(
            lane_ids == j, jnp.sum(sums[j], axis=1, keepdims=True), 0.0
        )
    partials[len(others)] = share * (1.0 / (ny * nz * nx))

    def part_copy(index):
        return pltpu.make_async_remote_copy(
            src_ref=partials.at[len(others)], dst_ref=partials.at[index],
            send_sem=part_send.at[index], recv_sem=part_recv.at[index],
            device_id=mate_id(*others[index]), device_id_type=MESH,
        )

    for index in range(len(others)):
        part_copy(index).start()
    for index in range(len(others)):
        part_copy(index).wait_recv()
    total = partials[0]
    for index in range(1, len(mates)):
        total = total + partials[index]
    totals[my_r] = total

    def total_copy(step, owner):
        return pltpu.make_async_remote_copy(
            src_ref=totals.at[my_r], dst_ref=totals.at[owner],
            send_sem=total_send.at[step], recv_sem=total_recv.at[step],
            device_id={"rve": turned(my_r, step, groups)}, device_id_type=MESH,
        )

    for step in range(1, groups):
        total_copy(step, my_r).start()
    for step in range(1, groups):
        total_copy(step, turned(my_r, -step, groups)).wait_recv()
    mine = tables[my_r]
    answer = jnp.zeros((8, 128), f32)
    for group in range(groups):
        for rank in range(CAP):
            chosen = (mine[:, TARGET : TARGET + 1] == float(group)) & (
                mine[:, RANK : RANK + 1] == float(rank)
            )
            line = totals[group, pl.ds(my_r * CAP + rank, 1), :]
            answer = answer + jnp.where(chosen, line, 0.0)
    rows_out[...] = answer[:listed, :strains]

    for step in range(1, groups):
        table_copy(step, my_r).wait_send()
        total_copy(step, my_r).wait_send()
    for index, (dy, dz) in enumerate(others):
        phase_copy(index, 0, 0).wait_send()
        force_copy(index, 0, 0).wait_send()
        part_copy(index).wait_send()
        for y in range(y_here):
            field_copy(dy, dz, y, my_load).wait_send()


def fused_body(strain, tangent, yield_list, destination, phase_map, polarization, stencil):
    groups, ngy, ngz = (lax.axis_size(name) for name in ("rve", "gy", "gz"))
    channels = polarization.shape[1]
    strains = polarization.shape[2]
    y_here, z_here, nx = polarization.shape[3:]
    ny, nz = y_here * ngy, z_here * ngz
    loads = groups * CAP
    count = ngy * ngz
    f32 = jnp.float32
    slot_rows = 3 * channels * nz
    vmem = pl.BlockSpec(memory_space=pltpu.VMEM)
    smem = pl.BlockSpec(memory_space=pltpu.SMEM)
    cell = pltpu.VMEM((ny, nz, nx), f32)
    vector = pltpu.VMEM((channels, ny, nz, nx), f32)

    def dma(*shape):
        return pltpu.SemaphoreType.DMA(shape)

    return pl.pallas_call(
        functools.partial(kernel, groups, ngy, ngz),
        out_shape=(
            jax.ShapeDtypeStruct((1, loads, channels, y_here, z_here, nx), f32),
            jax.ShapeDtypeStruct((yield_list.shape[0], strains), f32),
        ),
        in_specs=[smem, smem, smem, smem, smem, vmem, vmem],
        out_specs=(vmem, vmem),
        scratch_shapes=[
            pltpu.VMEM((groups, 8, 128), f32),
            pltpu.VMEM((loads, 128), f32),
            pltpu.VMEM((ny, nz, nx), jnp.int32),
            pltpu.VMEM((count, channels, y_here, z_here, nx), f32),
            vector,
            pltpu.VMEM((3 * channels * nz, 3 * slot_rows), jnp.bfloat16),
            pltpu.VMEM((2, (ny + 2) * slot_rows, 2 * nx), jnp.bfloat16),
            vector,
            vector,
            cell, cell, cell, cell,
            pltpu.VMEM((strains, loads, 128), f32),
            pltpu.VMEM((count, 8, 128), f32),
            pltpu.VMEM((groups, 8, 128), f32),
            dma(groups), dma(groups), dma(count), dma(count), dma(count), dma(count),
            dma(ngy, ngz, y_here), dma(ngy, ngz, y_here),
            dma(count), dma(count), dma(groups), dma(groups),
        ],
        compiler_params=pltpu.CompilerParams(
            collective_id=0, has_side_effects=True, vmem_limit_bytes=40 * 1024 * 1024
        ),
    )(strain, tangent, yield_list, destination, stencil, phase_map, polarization)


def body_for(mesh):
    def chosen(*arguments):
        strain, _, yield_list, _, phase_map, _, _ = arguments
        loads = lax.axis_size("rve") * CAP
        one_load_each = lax.axis_size("gy") * lax.axis_size("gz") == loads
        tiled = phase_map.shape[2] == 8 and phase_map.shape[3] == 128 and loads == 8
        if one_load_each and tiled and yield_list.shape[0] <= 8:
            return fused_body(*arguments)
        return body(*arguments)

    return chosen


def solution(mesh):
    return jax.shard_map(
        body_for(mesh),
        mesh=mesh,
        in_specs=(
            P("rve", None),
            P("rve"),
            P("rve"),
            P("rve", None),
            P("rve", "gy", "gz", None),
            P("rve", None, None, "gy", "gz", None),
            P(),
        ),
        out_specs=(P("rve", None, None, "gy", "gz", None), P("rve", None)),
        check_vma=False,
    )
```

```python
import functools

import jax
import jax.numpy as jnp
from jax import lax
from jax.experimental import pallas as pl
from jax.experimental.pallas import tpu as pltpu
from jax.sharding import PartitionSpec as P

CAP = 2
SWEEPS = 6
MESH = pl.DeviceIdType.MESH
TANGENT, TARGET, RANK, LISTED = 6, 7, 8, 9


FULL_PRECISION = lax.Precision.HIGHEST
LOWER_BOUND = 0.05
UPPER_BOUND = 1.95


def padded(block, sides, width):
    for axis, dim in sides:
        count = lax.axis_size(axis)
        forward = [(i, i + 1) for i in range(count - 1)]
        forward.append((count - 1, 0))
        backward = [(target, source) for source, target in forward]
        low = lax.ppermute(
            lax.slice_in_dim(block, block.shape[dim] - width, None, axis=dim), axis, forward
        )
        high = lax.ppermute(lax.slice_in_dim(block, 0, width, axis=dim), axis, backward)
        block = jnp.concatenate([low, block, high], axis=dim)
    return block


def chebyshev_weights(sweep_count):
    centre_value = 0.5 * (UPPER_BOUND + LOWER_BOUND)
    half_width = 0.5 * (UPPER_BOUND - LOWER_BOUND)
    ratio_value = centre_value / half_width
    rho_before = 1.0 / ratio_value
    weights = []
    for sweep_index in range(1, sweep_count):
        rho_after = 1.0 / (2.0 * ratio_value - rho_before)
        weights.append((rho_after * rho_before, 2.0 * rho_after / half_width))
        rho_before = rho_after
    return (1.0 / centre_value, weights)


def trim_margin(values_in, margin_have, margin_want, first_dim):
    excess = margin_have - margin_want
    values_in = lax.slice_in_dim(
        values_in, excess, values_in.shape[first_dim] - excess, axis=first_dim
    )
    return lax.slice_in_dim(
        values_in, excess, values_in.shape[first_dim + 1] - excess, axis=first_dim + 1
    )


def apply_stiffness(field_now, moduli, stencil):
    inner_y = field_now.shape[2] - 2
    inner_z = field_now.shape[3] - 2
    centre_mod = moduli[:, 1 : 1 + inner_y, 1 : 1 + inner_z, :]
    running = [None, None, None]
    for shift_y in (-1, 0, 1):
        for shift_z in (-1, 0, 1):
            shifted = field_now[
                :, :, 1 + shift_y : 1 + shift_y + inner_y, 1 + shift_z : 1 + shift_z + inner_z, :
            ]
            shifted_mod = moduli[
                :, 1 + shift_y : 1 + shift_y + inner_y, 1 + shift_z : 1 + shift_z + inner_z, :
            ]
            for shift_x in (-1, 0, 1):
                if shift_x != 0:
                    rolled = jnp.roll(shifted, -shift_x, axis=4)
                    rolled_mod = jnp.roll(shifted_mod, -shift_x, axis=3)
                else:
                    rolled = shifted
                    rolled_mod = shifted_mod
                offset_index = (shift_y + 1) * 9 + (shift_z + 1) * 3 + (shift_x + 1)
                edge_mod = 0.5 * (centre_mod + rolled_mod)
                weighted = [edge_mod * rolled[:, channel_in] for channel_in in range(3)]
                for channel_out in range(3):
                    mixed = stencil[channel_out, 0, offset_index] * weighted[0]
                    mixed = mixed + stencil[channel_out, 1, offset_index] * weighted[1]
                    mixed = mixed + stencil[channel_out, 2, offset_index] * weighted[2]
                    if running[channel_out] is None:
                        running[channel_out] = mixed
                    else:
                        running[channel_out] = running[channel_out] + mixed
    return jnp.stack(running, axis=1)


def body(strain, tangent, yield_list, destination, phase_map, polarization, stencil):
    groups = lax.axis_size("rve")
    rows_here = strain.shape[0]
    yield_count = yield_list.shape[0]
    picker = (jnp.arange(rows_here, dtype=jnp.int32)[None, :] == yield_list[:, None]).astype(
        jnp.float32
    )
    row_strain = jnp.dot(picker, strain, precision=FULL_PRECISION)
    row_tangent = jnp.dot(picker, tangent, precision=FULL_PRECISION)
    target = destination[:, 0]
    positions = jnp.arange(yield_count, dtype=jnp.int32)
    earlier = (target[:, None] == target[None, :]) & (positions[None, :] < positions[:, None])
    rank_in = jnp.sum(earlier.astype(jnp.int32), axis=1)
    group_ids = jnp.arange(groups, dtype=jnp.int32)
    slot_ids = jnp.arange(CAP, dtype=jnp.int32)
    onehot = (
        (target[None, None, :] == group_ids[:, None, None])
        & (rank_in[None, None, :] == slot_ids[None, :, None])
    ).astype(jnp.float32)
    packet = jnp.einsum("gci,ij->gcj", onehot, row_strain, precision=FULL_PRECISION)
    packet_tangent = (
        jnp.einsum("gci,i->gc", onehot, row_tangent, precision=FULL_PRECISION)
        + 1.0
        - jnp.sum(onehot, axis=2)
    )
    parcel = jnp.concatenate([packet, packet_tangent[:, :, None]], axis=2)
    arrived = lax.all_to_all(parcel, "rve", split_axis=0, concat_axis=0, tiled=True)
    slot_strain = arrived[:, :, :6].reshape(groups * CAP, 6)
    slot_tangent = arrived[:, :, 6].reshape(groups * CAP)
    phase_wide = padded(phase_map[0], (("gy", 0), ("gz", 1)), 2)
    moduli_wide = jnp.where(
        phase_wide[None] == 1, slot_tangent[:, None, None, None], jnp.float32(1.0)
    )
    moduli_core = trim_margin(moduli_wide, 2, 0, 1)
    moduli_one = trim_margin(moduli_wide, 2, 1, 1)
    polar_local = polarization[0]
    centre_diag = jnp.diagonal(stencil[:, :, 13])
    body_force = moduli_core[:, None] * jnp.einsum(
        "cjyzx,lj->lcyzx", polar_local, slot_strain, precision=FULL_PRECISION
    )
    inverse_diag = 1.0 / (centre_diag[None, :, None, None, None] * moduli_core[:, None])
    first_weight, weights = chebyshev_weights(SWEEPS)
    update = first_weight * (body_force * inverse_diag)
    field_now = update
    for old_weight, new_weight in weights:
        wrapped = padded(field_now, (("gy", 2), ("gz", 3)), 1)
        residual_now = body_force - apply_stiffness(wrapped, moduli_one, stencil)
        update = old_weight * update + new_weight * (residual_now * inverse_diag)
        field_now = field_now + update
    coupled = jnp.einsum(
        "cjyzx,lcyzx->lj", polar_local, moduli_core[:, None] * field_now, precision=FULL_PRECISION
    )
    partial_value = coupled + slot_strain * jnp.sum(moduli_core, axis=(1, 2, 3))[:, None]
    total_cells = (
        lax.axis_size("gy")
        * lax.axis_size("gz")
        * field_now.shape[2]
        * field_now.shape[3]
        * field_now.shape[4]
    )
    summed = lax.psum(partial_value, ("gy", "gz")) / total_cells
    returned = lax.all_to_all(
        summed.reshape(groups, CAP, 6), "rve", split_axis=0, concat_axis=0, tiled=True
    )
    stress_rows = jnp.einsum("gci,gcj->ij", onehot, returned, precision=FULL_PRECISION)
    return (field_now[None], stress_rows)


def kernel(
    groups, ngy, ngz,
    strain, tangent, yield_list, destination, stencil, phase, polar,
    fields, rows_out,
    tables, slots, phase_all, force_out, force, matrix, spread, field_now, update,
    mod_mid, mod_low, mod_high, mod_inv, sums, partials, totals,
    table_send, table_recv, phase_send, phase_recv, force_send, force_recv,
    field_send, field_recv, part_send, part_recv, total_send, total_recv,
):
    f32, bf16 = jnp.float32, jnp.bfloat16
    channels, strains = polar.shape[1], polar.shape[2]
    y_here, z_here, nx = polar.shape[3:]
    ny, nz = y_here * ngy, z_here * ngz
    wide = channels * nz
    slot_rows = 3 * wide
    depth = 3 * slot_rows
    listed = yield_list.shape[0]
    loads = groups * CAP
    my_r, my_y, my_z = lax.axis_index("rve"), lax.axis_index("gy"), lax.axis_index("gz")
    my_load = my_y * ngz + my_z

    def turned(base, step, count):
        return lax.rem(base + step + count, count)

    mates = [(dy, dz) for dy in list(range(1, ngy)) + [0] for dz in list(range(1, ngz)) + [0]]
    others = [mate for mate in mates if mate != (0, 0)]

    def mate_id(dy, dz):
        return {"gy": turned(my_y, dy, ngy), "gz": turned(my_z, dz, ngz)}

    def block(dy, dz):
        y_at = turned(my_y, dy, ngy) * y_here
        z_at = pl.multiple_of(turned(my_z, dz, ngz) * z_here, 8)
        return pl.ds(y_at, y_here), pl.ds(z_at, z_here)

    barrier = pltpu.get_barrier_semaphore()
    for dy, dz in others:
        pl.semaphore_signal(barrier, inc=1, device_id=mate_id(dy, dz), device_id_type=MESH)
    for step in range(1, groups):
        pl.semaphore_signal(
            barrier, inc=1, device_id={"rve": turned(my_r, step, groups)}, device_id_type=MESH
        )

    row_ids = lax.broadcasted_iota(jnp.int32, (8, 128), 0)
    lane_ids = lax.broadcasted_iota(jnp.int32, (8, 128), 1)
    table = jnp.zeros((8, 128), f32)
    for i in range(listed):
        point, target = yield_list[i], destination[i, 0]
        rank = jnp.int32(0)
        for k in range(i):
            rank = rank + jnp.where(destination[k, 0] == target, 1, 0)
        values = [strain[point, j] for j in range(strains)]
        values += [tangent[point], target.astype(f32), rank.astype(f32), jnp.float32(1.0)]
        for j, value in enumerate(values):
            table = jnp.where((row_ids == i) & (lane_ids == j), value, table)
    tables[my_r] = table

    pl.semaphore_wait(barrier, len(others) + groups - 1)

    def table_copy(step, owner):
        return pltpu.make_async_remote_copy(
            src_ref=tables.at[my_r], dst_ref=tables.at[owner],
            send_sem=table_send.at[step], recv_sem=table_recv.at[step],
            device_id={"rve": turned(my_r, step, groups)}, device_id_type=MESH,
        )

    def phase_copy(index, dy, dz):
        y_at, z_at = block(dy, dz)
        to_y, to_z = others[index]
        return pltpu.make_async_remote_copy(
            src_ref=phase.at[0], dst_ref=phase_all.at[y_at, z_at],
            send_sem=phase_send.at[index], recv_sem=phase_recv.at[index],
            device_id=mate_id(to_y, to_z), device_id_type=MESH,
        )

    for step in range(1, groups):
        table_copy(step, my_r).start()
    for index in range(len(others)):
        phase_copy(index, 0, 0).start()
    own_y, own_z = block(0, 0)
    phase_all[own_y, own_z, :] = phase[0]

    for step in range(1, groups):
        table_copy(step, turned(my_r, -step, groups)).wait_recv()
    for source in range(groups):
        heard = tables[source]
        named = (heard[:, TARGET : TARGET + 1] == my_r.astype(f32)) & (
            heard[:, LISTED : LISTED + 1] == 1.0
        )
        for rank in range(CAP):
            chosen = named & (heard[:, RANK : RANK + 1] == float(rank))
            line = jnp.sum(jnp.where(chosen, heard, 0.0), axis=0, keepdims=True)
            missing = 1.0 - line[:, LISTED : LISTED + 1]
            line = line + jnp.where(lane_ids[:1] == TANGENT, missing, 0.0)
            at = source * CAP + rank
            slots[at : at + 1, :] = line

    def slot_value(load, index):
        return jnp.broadcast_to(slots[pl.ds(load, 1), :][:, index : index + 1], (8, 128))

    def force_copy(index, dy, dz):
        y_at, z_at = block(dy, dz)
        return pltpu.make_async_remote_copy(
            src_ref=force_out.at[index], dst_ref=force.at[:, y_at, z_at],
            send_sem=force_send.at[index], recv_sem=force_recv.at[index],
            device_id=mate_id(*others[index]), device_id_type=MESH,
        )

    for index, (dy, dz) in enumerate(mates):
        load = turned(my_y, dy, ngy) * ngz + turned(my_z, dz, ngz)
        strain_of = [slot_value(load, j) for j in range(strains)]
        for c in range(channels):
            for y in range(y_here):
                value = polar[0, c, 0, y] * strain_of[0]
                for j in range(1, strains):
                    value = value + polar[0, c, j, y] * strain_of[j]
                if (dy, dz) == (0, 0):
                    force[c, my_y * y_here + y, own_z, :] = value
                else:
                    force_out[index, c, y] = value
        if (dy, dz) != (0, 0):
            force_copy(index, 0, 0).start()

    column = lax.broadcasted_iota(jnp.int32, (1, depth), 1)
    column_y = column // slot_rows
    column_kind = lax.rem(column, slot_rows) // wide
    column_d = lax.rem(column, wide) // nz
    picks = [[(column_y == dy) & (column_d == d) for d in range(channels)] for dy in range(3)]
    z_row = lax.broadcasted_iota(jnp.int32, (nz, depth), 0)
    z_column = lax.rem(lax.broadcasted_iota(jnp.int32, (nz, depth), 1), nz)
    bands = [z_column == lax.rem(z_row + dz - 1 + nz, nz) for dz in range(3)]
    is_low = jnp.broadcast_to(column_kind, (nz, depth)) == 1
    for dx in range(3):
        for c in range(channels):
            values = jnp.zeros((nz, depth), f32)
            for dz in range(3):
                line = jnp.zeros((1, depth), f32)
                for dy in range(3):
                    for d in range(channels):
                        line = jnp.where(
                            picks[dy][d], 0.5 * stencil[c, d, dy * 9 + dz * 3 + dx], line
                        )
                values = values + jnp.where(bands[dz], line, 0.0)
            high = values.astype(bf16).astype(f32)
            low = values - high
            at = (dx * channels + c) * nz
            matrix[at : at + nz, :] = jnp.where(is_low, low, high).astype(bf16)

    for index, (dy, dz) in enumerate(others):
        phase_copy(index, -dy, -dz).wait_recv()
    tangent_row = slots[pl.ds(my_load, 1), :][:, TANGENT : TANGENT + 1]
    my_tangent = jnp.broadcast_to(tangent_row, (nz, nx))
    inverse_tangent = 1.0 / my_tangent
    for y in range(ny):
        second = phase_all[y] == 1
        mod = jnp.where(second, my_tangent, 1.0)
        mod_mid[y] = mod
        mod_low[y] = pltpu.roll(mod, nx - 1, 1)
        mod_high[y] = pltpu.roll(mod, 1, 1)
        mod_inv[y] = jnp.where(second, inverse_tangent, 1.0)
    ones = jnp.ones((nz, nx), f32)
    inverse_centre = [1.0 / (ones * stencil[c, c, 13]) for c in range(channels)]

    def put(buffer, y, c, value):
        both = jnp.concatenate([value, value * mod_mid[y]], axis=1)
        high = both.astype(bf16)
        low = (both - high.astype(f32)).astype(bf16)
        at = pl.multiple_of((y + 1) * slot_rows + c * nz, 16)
        spread[buffer, pl.ds(at, nz), :] = high
        spread[buffer, pl.ds(at + wide, nz), :] = high
        spread[buffer, pl.ds(at + 2 * wide, nz), :] = low

    def wrap(buffer):
        spread[buffer, 0:slot_rows, :] = spread[buffer, ny * slot_rows : (ny + 1) * slot_rows, :]
        spread[buffer, (ny + 1) * slot_rows : (ny + 2) * slot_rows, :] = spread[
            buffer, slot_rows : 2 * slot_rows, :
        ]

    for index, (dy, dz) in enumerate(others):
        force_copy(index, -dy, -dz).wait_recv()
    first_weight, weights = chebyshev_weights(SWEEPS)
    for y in range(ny):
        for c in range(channels):
            value = first_weight * (force[c, y] * inverse_centre[c])
            update[c, y] = value
            field_now[c, y] = value
            put(0, y, c, value)
    wrap(0)

    def row_product(buffer, y):
        at = y * slot_rows if isinstance(y, int) else pl.multiple_of(y * slot_rows, 16)
        return jnp.dot(
            matrix[...], spread[buffer, pl.ds(at, depth), :], preferred_element_type=f32
        )

    def finish_row(product, buffer, y, old_weight, new_weight, last):
        for c in range(channels):
            parts = []
            for dx, mod in enumerate((mod_low, mod_mid, mod_high)):
                row = (dx * channels + c) * nz
                parts.append(
                    mod[y] * product[row : row + nz, :nx] + product[row : row + nz, nx:]
                )
            stiff = parts[1] + pltpu.roll(parts[0], 1, 1) + pltpu.roll(parts[2], nx - 1, 1)
            residual = (force[c, y] - stiff * mod_inv[y]) * inverse_centre[c]
            step = old_weight * update[c, y] + new_weight * residual
            value = field_now[c, y] + step
            field_now[c, y] = value
            if not last:
                update[c, y] = step
                put(1 - buffer, y, c, value)

    def sweep_pair(pair, carry):
        for buffer in range(2):
            k = pair * 2 + buffer
            old_weight, new_weight = jnp.float32(weights[0][0]), jnp.float32(weights[0][1])
            for position in range(1, len(weights) - 1):
                old_weight = jnp.where(k == position, weights[position][0], old_weight)
                new_weight = jnp.where(k == position, weights[position][1], new_weight)
            for y in range(ny):
                finish_row(row_product(buffer, y), buffer, y, old_weight, new_weight, False)
            wrap(1 - buffer)
        return carry

    assert len(weights) % 2 == 1
    lax.fori_loop(0, (len(weights) - 1) // 2, sweep_pair, 0)

    def field_copy(dy, dz, y, load):
        to_y, to_z = turned(my_y, dy, ngy), turned(my_z, dz, ngz)
        z_at = pl.ds(pl.multiple_of(to_z * z_here, 8), z_here)
        return pltpu.make_async_remote_copy(
            src_ref=field_now.at[:, to_y * y_here + y, z_at],
            dst_ref=fields.at[0, load, :, y],
            send_sem=field_send.at[dy, dz, y], recv_sem=field_recv.at[dy, dz, y],
            device_id={"gy": to_y, "gz": to_z}, device_id_type=MESH,
        )

    final_buffer = (len(weights) - 1) % 2
    last_rows = [
        (dy, y, turned(my_y, dy, ngy) * y_here + y)
        for dy in list(range(1, ngy)) + [0]
        for y in range(y_here)
    ]
    product = row_product(final_buffer, last_rows[0][2])
    for place, (dy, y, row) in enumerate(last_rows):
        later = None
        if place + 1 < len(last_rows):
            later = row_product(final_buffer, last_rows[place + 1][2])
        finish_row(product, final_buffer, row, weights[-1][0], weights[-1][1], True)
        product = later
        for dz in list(range(1, ngz)) + [0]:
            if (dy, dz) != (0, 0):
                field_copy(dy, dz, y, my_load).start()
            else:
                for c in range(channels):
                    fields[0, my_load, c, y] = field_now[c, row, own_z, :]

    seconds = [phase[0, y] == 1 for y in range(y_here)]
    for dy, dz in mates:
        load = turned(my_y, -dy, ngy) * ngz + turned(my_z, -dz, ngz)
        if (dy, dz) != (0, 0):
            for y in range(y_here):
                field_copy(dy, dz, y, load).wait_recv()
        slope = slot_value(load, TANGENT)
        totals_of = [jnp.zeros((8, 128), f32) for _ in range(strains)]
        for y in range(y_here):
            mod = jnp.where(seconds[y], slope, 1.0)
            for c in range(channels):
                flux = mod * fields[0, load, c, y]
                for j in range(strains):
                    totals_of[j] = totals_of[j] + polar[0, c, j, y] * flux
        for j in range(strains):
            sums[j, pl.ds(load, 1), :] = jnp.sum(totals_of[j], axis=0, keepdims=True)
    ones_here = jnp.zeros((8, 128), f32)
    for y in range(y_here):
        ones_here = ones_here + jnp.where(seconds[y], 1.0, 0.0)
    second_count = jnp.sum(jnp.sum(ones_here, axis=0, keepdims=True), axis=1, keepdims=True)
    slot_table = slots[...]
    mod_sum = second_count * slot_table[:, TANGENT : TANGENT + 1] + (
        float(y_here * z_here * nx) - second_count
    )
    share = jnp.where(lane_ids < strains, slot_table * mod_sum, 0.0)
    for j in range(strains):
        share = share + jnp.where(
            lane_ids == j, jnp.sum(sums[j], axis=1, keepdims=True), 0.0
        )
    partials[len(others)] = share * (1.0 / (ny * nz * nx))

    def part_copy(index):
        return pltpu.make_async_remote_copy(
            src_ref=partials.at[len(others)], dst_ref=partials.at[index],
            send_sem=part_send.at[index], recv_sem=part_recv.at[index],
            device_id=mate_id(*others[index]), device_id_type=MESH,
        )

    for index in range(len(others)):
        part_copy(index).start()
    for index in range(len(others)):
        part_copy(index).wait_recv()
    total = partials[0]
    for index in range(1, len(mates)):
        total = total + partials[index]
    totals[my_r] = total

    def total_copy(step, owner):
        return pltpu.make_async_remote_copy(
            src_ref=totals.at[my_r], dst_ref=totals.at[owner],
            send_sem=total_send.at[step], recv_sem=total_recv.at[step],
            device_id={"rve": turned(my_r, step, groups)}, device_id_type=MESH,
        )

    for step in range(1, groups):
        total_copy(step, my_r).start()
    for step in range(1, groups):
        total_copy(step, turned(my_r, -step, groups)).wait_recv()
    mine = tables[my_r]
    answer = jnp.zeros((8, 128), f32)
    for group in range(groups):
        for rank in range(CAP):
            chosen = (mine[:, TARGET : TARGET + 1] == float(group)) & (
                mine[:, RANK : RANK + 1] == float(rank)
            )
            line = totals[group, pl.ds(my_r * CAP + rank, 1), :]
            answer = answer + jnp.where(chosen, line, 0.0)
    rows_out[...] = answer[:listed, :strains]

    for step in range(1, groups):
        table_copy(step, my_r).wait_send()
        total_copy(step, my_r).wait_send()
    for index, (dy, dz) in enumerate(others):
        phase_copy(index, 0, 0).wait_send()
        force_copy(index, 0, 0).wait_send()
        part_copy(index).wait_send()
        for y in range(y_here):
            field_copy(dy, dz, y, my_load).wait_send()


def fused_body(strain, tangent, yield_list, destination, phase_map, polarization, stencil):
    groups, ngy, ngz = (lax.axis_size(name) for name in ("rve", "gy", "gz"))
    channels = polarization.shape[1]
    strains = polarization.shape[2]
    y_here, z_here, nx = polarization.shape[3:]
    ny, nz = y_here * ngy, z_here * ngz
    loads = groups * CAP
    count = ngy * ngz
    f32 = jnp.float32
    slot_rows = 3 * channels * nz
    vmem = pl.BlockSpec(memory_space=pltpu.VMEM)
    smem = pl.BlockSpec(memory_space=pltpu.SMEM)
    cell = pltpu.VMEM((ny, nz, nx), f32)
    vector = pltpu.VMEM((channels, ny, nz, nx), f32)

    def dma(*shape):
        return pltpu.SemaphoreType.DMA(shape)

    return pl.pallas_call(
        functools.partial(kernel, groups, ngy, ngz),
        out_shape=(
            jax.ShapeDtypeStruct((1, loads, channels, y_here, z_here, nx), f32),
            jax.ShapeDtypeStruct((yield_list.shape[0], strains), f32),
        ),
        in_specs=[smem, smem, smem, smem, smem, vmem, vmem],
        out_specs=(vmem, vmem),
        scratch_shapes=[
            pltpu.VMEM((groups, 8, 128), f32),
            pltpu.VMEM((loads, 128), f32),
            pltpu.VMEM((ny, nz, nx), jnp.int32),
            pltpu.VMEM((count, channels, y_here, z_here, nx), f32),
            vector,
            pltpu.VMEM((3 * channels * nz, 3 * slot_rows), jnp.bfloat16),
            pltpu.VMEM((2, (ny + 2) * slot_rows, 2 * nx), jnp.bfloat16),
            vector,
            vector,
            cell, cell, cell, cell,
            pltpu.VMEM((strains, loads, 128), f32),
            pltpu.VMEM((count, 8, 128), f32),
            pltpu.VMEM((groups, 8, 128), f32),
            dma(groups), dma(groups), dma(count), dma(count), dma(count), dma(count),
            dma(ngy, ngz, y_here), dma(ngy, ngz, y_here),
            dma(count), dma(count), dma(groups), dma(groups),
        ],
        compiler_params=pltpu.CompilerParams(
            collective_id=0, has_side_effects=True, vmem_limit_bytes=40 * 1024 * 1024
        ),
    )(strain, tangent, yield_list, destination, stencil, phase_map, polarization)


def body_for(mesh):
    def chosen(*arguments):
        strain, _, yield_list, _, phase_map, _, _ = arguments
        loads = lax.axis_size("rve") * CAP
        one_load_each = lax.axis_size("gy") * lax.axis_size("gz") == loads
        tiled = phase_map.shape[2] == 8 and phase_map.shape[3] == 128 and loads == 8
        if one_load_each and tiled and yield_list.shape[0] <= 8:
            return fused_body(*arguments)
        return body(*arguments)

    return chosen


def solution(mesh):
    return jax.shard_map(
        body_for(mesh),
        mesh=mesh,
        in_specs=(
            P("rve", None),
            P("rve"),
            P("rve"),
            P("rve", None),
            P("rve", "gy", "gz", None),
            P("rve", None, None, "gy", "gz", None),
            P(),
        ),
        out_specs=(P("rve", None, None, "gy", "gz", None), P("rve", None)),
        check_vma=False,
    )
```

```python
import functools

import jax
import jax.numpy as jnp
from jax import lax
from jax.experimental import pallas as pl
from jax.experimental.pallas import tpu as pltpu
from jax.sharding import PartitionSpec as P

CAP = 2
SWEEPS = 6
MESH = pl.DeviceIdType.MESH
TANGENT, TARGET, RANK, LISTED = 6, 7, 8, 9


FULL_PRECISION = lax.Precision.HIGHEST
LOWER_BOUND = 0.05
UPPER_BOUND = 1.95


def padded(block, sides, width):
    for axis, dim in sides:
        count = lax.axis_size(axis)
        forward = [(i, i + 1) for i in range(count - 1)]
        forward.append((count - 1, 0))
        backward = [(target, source) for source, target in forward]
        low = lax.ppermute(
            lax.slice_in_dim(block, block.shape[dim] - width, None, axis=dim), axis, forward
        )
        high = lax.ppermute(lax.slice_in_dim(block, 0, width, axis=dim), axis, backward)
        block = jnp.concatenate([low, block, high], axis=dim)
    return block


def chebyshev_weights(sweep_count):
    centre_value = 0.5 * (UPPER_BOUND + LOWER_BOUND)
    half_width = 0.5 * (UPPER_BOUND - LOWER_BOUND)
    ratio_value = centre_value / half_width
    rho_before = 1.0 / ratio_value
    weights = []
    for sweep_index in range(1, sweep_count):
        rho_after = 1.0 / (2.0 * ratio_value - rho_before)
        weights.append((rho_after * rho_before, 2.0 * rho_after / half_width))
        rho_before = rho_after
    return (1.0 / centre_value, weights)


def trim_margin(values_in, margin_have, margin_want, first_dim):
    excess = margin_have - margin_want
    values_in = lax.slice_in_dim(
        values_in, excess, values_in.shape[first_dim] - excess, axis=first_dim
    )
    return lax.slice_in_dim(
        values_in, excess, values_in.shape[first_dim + 1] - excess, axis=first_dim + 1
    )


def apply_stiffness(field_now, moduli, stencil):
    inner_y = field_now.shape[2] - 2
    inner_z = field_now.shape[3] - 2
    centre_mod = moduli[:, 1 : 1 + inner_y, 1 : 1 + inner_z, :]
    running = [None, None, None]
    for shift_y in (-1, 0, 1):
        for shift_z in (-1, 0, 1):
            shifted = field_now[
                :, :, 1 + shift_y : 1 + shift_y + inner_y, 1 + shift_z : 1 + shift_z + inner_z, :
            ]
            shifted_mod = moduli[
                :, 1 + shift_y : 1 + shift_y + inner_y, 1 + shift_z : 1 + shift_z + inner_z, :
            ]
            for shift_x in (-1, 0, 1):
                if shift_x != 0:
                    rolled = jnp.roll(shifted, -shift_x, axis=4)
                    rolled_mod = jnp.roll(shifted_mod, -shift_x, axis=3)
                else:
                    rolled = shifted
                    rolled_mod = shifted_mod
                offset_index = (shift_y + 1) * 9 + (shift_z + 1) * 3 + (shift_x + 1)
                edge_mod = 0.5 * (centre_mod + rolled_mod)
                weighted = [edge_mod * rolled[:, channel_in] for channel_in in range(3)]
                for channel_out in range(3):
                    mixed = stencil[channel_out, 0, offset_index] * weighted[0]
                    mixed = mixed + stencil[channel_out, 1, offset_index] * weighted[1]
                    mixed = mixed + stencil[channel_out, 2, offset_index] * weighted[2]
                    if running[channel_out] is None:
                        running[channel_out] = mixed
                    else:
                        running[channel_out] = running[channel_out] + mixed
    return jnp.stack(running, axis=1)


def body(strain, tangent, yield_list, destination, phase_map, polarization, stencil):
    groups = lax.axis_size("rve")
    rows_here = strain.shape[0]
    yield_count = yield_list.shape[0]
    picker = (jnp.arange(rows_here, dtype=jnp.int32)[None, :] == yield_list[:, None]).astype(
        jnp.float32
    )
    row_strain = jnp.dot(picker, strain, precision=FULL_PRECISION)
    row_tangent = jnp.dot(picker, tangent, precision=FULL_PRECISION)
    target = destination[:, 0]
    positions = jnp.arange(yield_count, dtype=jnp.int32)
    earlier = (target[:, None] == target[None, :]) & (positions[None, :] < positions[:, None])
    rank_in = jnp.sum(earlier.astype(jnp.int32), axis=1)
    group_ids = jnp.arange(groups, dtype=jnp.int32)
    slot_ids = jnp.arange(CAP, dtype=jnp.int32)
    onehot = (
        (target[None, None, :] == group_ids[:, None, None])
        & (rank_in[None, None, :] == slot_ids[None, :, None])
    ).astype(jnp.float32)
    packet = jnp.einsum("gci,ij->gcj", onehot, row_strain, precision=FULL_PRECISION)
    packet_tangent = (
        jnp.einsum("gci,i->gc", onehot, row_tangent, precision=FULL_PRECISION)
        + 1.0
        - jnp.sum(onehot, axis=2)
    )
    parcel = jnp.concatenate([packet, packet_tangent[:, :, None]], axis=2)
    arrived = lax.all_to_all(parcel, "rve", split_axis=0, concat_axis=0, tiled=True)
    slot_strain = arrived[:, :, :6].reshape(groups * CAP, 6)
    slot_tangent = arrived[:, :, 6].reshape(groups * CAP)
    phase_wide = padded(phase_map[0], (("gy", 0), ("gz", 1)), 2)
    moduli_wide = jnp.where(
        phase_wide[None] == 1, slot_tangent[:, None, None, None], jnp.float32(1.0)
    )
    moduli_core = trim_margin(moduli_wide, 2, 0, 1)
    moduli_one = trim_margin(moduli_wide, 2, 1, 1)
    polar_local = polarization[0]
    centre_diag = jnp.diagonal(stencil[:, :, 13])
    body_force = moduli_core[:, None] * jnp.einsum(
        "cjyzx,lj->lcyzx", polar_local, slot_strain, precision=FULL_PRECISION
    )
    inverse_diag = 1.0 / (centre_diag[None, :, None, None, None] * moduli_core[:, None])
    first_weight, weights = chebyshev_weights(SWEEPS)
    update = first_weight * (body_force * inverse_diag)
    field_now = update
    for old_weight, new_weight in weights:
        wrapped = padded(field_now, (("gy", 2), ("gz", 3)), 1)
        residual_now = body_force - apply_stiffness(wrapped, moduli_one, stencil)
        update = old_weight * update + new_weight * (residual_now * inverse_diag)
        field_now = field_now + update
    coupled = jnp.einsum(
        "cjyzx,lcyzx->lj", polar_local, moduli_core[:, None] * field_now, precision=FULL_PRECISION
    )
    partial_value = coupled + slot_strain * jnp.sum(moduli_core, axis=(1, 2, 3))[:, None]
    total_cells = (
        lax.axis_size("gy")
        * lax.axis_size("gz")
        * field_now.shape[2]
        * field_now.shape[3]
        * field_now.shape[4]
    )
    summed = lax.psum(partial_value, ("gy", "gz")) / total_cells
    returned = lax.all_to_all(
        summed.reshape(groups, CAP, 6), "rve", split_axis=0, concat_axis=0, tiled=True
    )
    stress_rows = jnp.einsum("gci,gcj->ij", onehot, returned, precision=FULL_PRECISION)
    return (field_now[None], stress_rows)


def kernel(
    groups, ngy, ngz,
    strain, tangent, yield_list, destination, stencil, phase, polar,
    fields, rows_out,
    tables, slots, phase_all, force_out, force, matrix, spread, field_now, update,
    mod_mid, mod_low, mod_high, mod_inv, sums, partials, totals,
    table_send, table_recv, phase_send, phase_recv, force_send, force_recv,
    field_send, field_recv, part_send, part_recv, total_send, total_recv,
):
    f32, bf16 = jnp.float32, jnp.bfloat16
    channels, strains = polar.shape[1], polar.shape[2]
    y_here, z_here, nx = polar.shape[3:]
    ny, nz = y_here * ngy, z_here * ngz
    wide = channels * nz
    slot_rows = 3 * wide
    depth = 3 * slot_rows
    listed = yield_list.shape[0]
    loads = groups * CAP
    my_r, my_y, my_z = lax.axis_index("rve"), lax.axis_index("gy"), lax.axis_index("gz")
    my_load = my_y * ngz + my_z

    def turned(base, step, count):
        return lax.rem(base + step + count, count)

    mates = [(dy, dz) for dy in list(range(1, ngy)) + [0] for dz in list(range(1, ngz)) + [0]]
    others = [mate for mate in mates if mate != (0, 0)]

    def mate_id(dy, dz):
        return {"gy": turned(my_y, dy, ngy), "gz": turned(my_z, dz, ngz)}

    def block(dy, dz):
        y_at = turned(my_y, dy, ngy) * y_here
        z_at = pl.multiple_of(turned(my_z, dz, ngz) * z_here, 8)
        return pl.ds(y_at, y_here), pl.ds(z_at, z_here)

    barrier = pltpu.get_barrier_semaphore()
    for dy, dz in others:
        pl.semaphore_signal(barrier, inc=1, device_id=mate_id(dy, dz), device_id_type=MESH)
    for step in range(1, groups):
        pl.semaphore_signal(
            barrier, inc=1, device_id={"rve": turned(my_r, step, groups)}, device_id_type=MESH
        )

    row_ids = lax.broadcasted_iota(jnp.int32, (8, 128), 0)
    lane_ids = lax.broadcasted_iota(jnp.int32, (8, 128), 1)
    table = jnp.zeros((8, 128), f32)
    for i in range(listed):
        point, target = yield_list[i], destination[i, 0]
        rank = jnp.int32(0)
        for k in range(i):
            rank = rank + jnp.where(destination[k, 0] == target, 1, 0)
        values = [strain[point, j] for j in range(strains)]
        values += [tangent[point], target.astype(f32), rank.astype(f32), jnp.float32(1.0)]
        for j, value in enumerate(values):
            table = jnp.where((row_ids == i) & (lane_ids == j), value, table)
    tables[my_r] = table

    pl.semaphore_wait(barrier, len(others) + groups - 1)

    def table_copy(step, owner):
        return pltpu.make_async_remote_copy(
            src_ref=tables.at[my_r], dst_ref=tables.at[owner],
            send_sem=table_send.at[step], recv_sem=table_recv.at[step],
            device_id={"rve": turned(my_r, step, groups)}, device_id_type=MESH,
        )

    def phase_copy(index, dy, dz):
        y_at, z_at = block(dy, dz)
        to_y, to_z = others[index]
        return pltpu.make_async_remote_copy(
            src_ref=phase.at[0], dst_ref=phase_all.at[y_at, z_at],
            send_sem=phase_send.at[index], recv_sem=phase_recv.at[index],
            device_id=mate_id(to_y, to_z), device_id_type=MESH,
        )

    for step in range(1, groups):
        table_copy(step, my_r).start()
    for index in range(len(others)):
        phase_copy(index, 0, 0).start()
    own_y, own_z = block(0, 0)
    phase_all[own_y, own_z, :] = phase[0]

    for step in range(1, groups):
        table_copy(step, turned(my_r, -step, groups)).wait_recv()
    for source in range(groups):
        heard = tables[source]
        named = (heard[:, TARGET : TARGET + 1] == my_r.astype(f32)) & (
            heard[:, LISTED : LISTED + 1] == 1.0
        )
        for rank in range(CAP):
            chosen = named & (heard[:, RANK : RANK + 1] == float(rank))
            line = jnp.sum(jnp.where(chosen, heard, 0.0), axis=0, keepdims=True)
            missing = 1.0 - line[:, LISTED : LISTED + 1]
            line = line + jnp.where(lane_ids[:1] == TANGENT, missing, 0.0)
            at = source * CAP + rank
            slots[at : at + 1, :] = line

    def slot_value(load, index):
        return jnp.broadcast_to(slots[pl.ds(load, 1), :][:, index : index + 1], (8, 128))

    def force_copy(index, dy, dz):
        y_at, z_at = block(dy, dz)
        return pltpu.make_async_remote_copy(
            src_ref=force_out.at[index], dst_ref=force.at[:, y_at, z_at],
            send_sem=force_send.at[index], recv_sem=force_recv.at[index],
            device_id=mate_id(*others[index]), device_id_type=MESH,
        )

    for index, (dy, dz) in enumerate(mates):
        load = turned(my_y, dy, ngy) * ngz + turned(my_z, dz, ngz)
        strain_of = [slot_value(load, j) for j in range(strains)]
        for c in range(channels):
            for y in range(y_here):
                value = polar[0, c, 0, y] * strain_of[0]
                for j in range(1, strains):
                    value = value + polar[0, c, j, y] * strain_of[j]
                if (dy, dz) == (0, 0):
                    force[c, my_y * y_here + y, own_z, :] = value
                else:
                    force_out[index, c, y] = value
        if (dy, dz) != (0, 0):
            force_copy(index, 0, 0).start()

    column = lax.broadcasted_iota(jnp.int32, (1, depth), 1)
    column_y = column // slot_rows
    column_kind = lax.rem(column, slot_rows) // wide
    column_d = lax.rem(column, wide) // nz
    picks = [[(column_y == dy) & (column_d == d) for d in range(channels)] for dy in range(3)]
    z_row = lax.broadcasted_iota(jnp.int32, (nz, depth), 0)
    z_column = lax.rem(lax.broadcasted_iota(jnp.int32, (nz, depth), 1), nz)
    bands = [z_column == lax.rem(z_row + dz - 1 + nz, nz) for dz in range(3)]
    is_low = jnp.broadcast_to(column_kind, (nz, depth)) == 1
    for dx in range(3):
        for c in range(channels):
            values = jnp.zeros((nz, depth), f32)
            for dz in range(3):
                line = jnp.zeros((1, depth), f32)
                for dy in range(3):
                    for d in range(channels):
                        line = jnp.where(
                            picks[dy][d], 0.5 * stencil[c, d, dy * 9 + dz * 3 + dx], line
                        )
                values = values + jnp.where(bands[dz], line, 0.0)
            high = values.astype(bf16).astype(f32)
            low = values - high
            at = (dx * channels + c) * nz
            matrix[at : at + nz, :] = jnp.where(is_low, low, high).astype(bf16)

    for index, (dy, dz) in enumerate(others):
        phase_copy(index, -dy, -dz).wait_recv()
    tangent_row = slots[pl.ds(my_load, 1), :][:, TANGENT : TANGENT + 1]
    my_tangent = jnp.broadcast_to(tangent_row, (nz, nx))
    inverse_tangent = 1.0 / my_tangent
    for y in range(ny):
        second = phase_all[y] == 1
        mod = jnp.where(second, my_tangent, 1.0)
        mod_mid[y] = mod
        mod_low[y] = pltpu.roll(mod, nx - 1, 1)
        mod_high[y] = pltpu.roll(mod, 1, 1)
        mod_inv[y] = jnp.where(second, inverse_tangent, 1.0)
    ones = jnp.ones((nz, nx), f32)
    inverse_centre = [1.0 / (ones * stencil[c, c, 13]) for c in range(channels)]

    def put(buffer, y, c, value):
        both = jnp.concatenate([value, value * mod_mid[y]], axis=1)
        high = both.astype(bf16)
        low = (both - high.astype(f32)).astype(bf16)
        at = pl.multiple_of((y + 1) * slot_rows + c * nz, 16)
        spread[buffer, pl.ds(at, nz), :] = high
        spread[buffer, pl.ds(at + wide, nz), :] = high
        spread[buffer, pl.ds(at + 2 * wide, nz), :] = low

    def wrap(buffer):
        spread[buffer, 0:slot_rows, :] = spread[buffer, ny * slot_rows : (ny + 1) * slot_rows, :]
        spread[buffer, (ny + 1) * slot_rows : (ny + 2) * slot_rows, :] = spread[
            buffer, slot_rows : 2 * slot_rows, :
        ]

    for index, (dy, dz) in enumerate(others):
        force_copy(index, -dy, -dz).wait_recv()
    first_weight, weights = chebyshev_weights(SWEEPS)
    for y in range(ny):
        for c in range(channels):
            value = first_weight * (force[c, y] * inverse_centre[c])
            update[c, y] = value
            field_now[c, y] = value
            put(0, y, c, value)
    wrap(0)

    def row_product(buffer, y):
        at = y * slot_rows if isinstance(y, int) else pl.multiple_of(y * slot_rows, 16)
        return jnp.dot(
            matrix[...], spread[buffer, pl.ds(at, depth), :], preferred_element_type=f32
        )

    def finish_row(product, buffer, y, old_weight, new_weight, last):
        for c in range(channels):
            parts = []
            for dx, mod in enumerate((mod_low, mod_mid, mod_high)):
                row = (dx * channels + c) * nz
                parts.append(
                    mod[y] * product[row : row + nz, :nx] + product[row : row + nz, nx:]
                )
            stiff = parts[1] + pltpu.roll(parts[0], 1, 1) + pltpu.roll(parts[2], nx - 1, 1)
            residual = (force[c, y] - stiff * mod_inv[y]) * inverse_centre[c]
            step = old_weight * update[c, y] + new_weight * residual
            value = field_now[c, y] + step
            field_now[c, y] = value
            if not last:
                update[c, y] = step
                put(1 - buffer, y, c, value)

    def sweep_pair(pair, carry):
        for buffer in range(2):
            k = pair * 2 + buffer
            old_weight, new_weight = jnp.float32(weights[0][0]), jnp.float32(weights[0][1])
            for position in range(1, len(weights) - 1):
                old_weight = jnp.where(k == position, weights[position][0], old_weight)
                new_weight = jnp.where(k == position, weights[position][1], new_weight)
            product = row_product(buffer, 0)
            for y in range(ny):
                later = row_product(buffer, y + 1) if y + 1 < ny else None
                finish_row(product, buffer, y, old_weight, new_weight, False)
                product = later
            wrap(1 - buffer)
        return carry

    assert len(weights) % 2 == 1
    lax.fori_loop(0, (len(weights) - 1) // 2, sweep_pair, 0)

    def field_copy(dy, dz, y, load):
        to_y, to_z = turned(my_y, dy, ngy), turned(my_z, dz, ngz)
        z_at = pl.ds(pl.multiple_of(to_z * z_here, 8), z_here)
        return pltpu.make_async_remote_copy(
            src_ref=field_now.at[:, to_y * y_here + y, z_at],
            dst_ref=fields.at[0, load, :, y],
            send_sem=field_send.at[dy, dz, y], recv_sem=field_recv.at[dy, dz, y],
            device_id={"gy": to_y, "gz": to_z}, device_id_type=MESH,
        )

    final_buffer = (len(weights) - 1) % 2
    last_rows = [
        (dy, y, turned(my_y, dy, ngy) * y_here + y)
        for dy in list(range(1, ngy)) + [0]
        for y in range(y_here)
    ]
    product = row_product(final_buffer, last_rows[0][2])
    for place, (dy, y, row) in enumerate(last_rows):
        later = None
        if place + 1 < len(last_rows):
            later = row_product(final_buffer, last_rows[place + 1][2])
        finish_row(product, final_buffer, row, weights[-1][0], weights[-1][1], True)
        product = later
        for dz in list(range(1, ngz)) + [0]:
            if (dy, dz) != (0, 0):
                field_copy(dy, dz, y, my_load).start()
            else:
                for c in range(channels):
                    fields[0, my_load, c, y] = field_now[c, row, own_z, :]

    seconds = [phase[0, y] == 1 for y in range(y_here)]
    for dy, dz in mates:
        load = turned(my_y, -dy, ngy) * ngz + turned(my_z, -dz, ngz)
        if (dy, dz) != (0, 0):
            for y in range(y_here):
                field_copy(dy, dz, y, load).wait_recv()
        slope = slot_value(load, TANGENT)
        totals_of = [jnp.zeros((8, 128), f32) for _ in range(strains)]
        for y in range(y_here):
            mod = jnp.where(seconds[y], slope, 1.0)
            for c in range(channels):
                flux = mod * fields[0, load, c, y]
                for j in range(strains):
                    totals_of[j] = totals_of[j] + polar[0, c, j, y] * flux
        for j in range(strains):
            sums[j, pl.ds(load, 1), :] = jnp.sum(totals_of[j], axis=0, keepdims=True)
    ones_here = jnp.zeros((8, 128), f32)
    for y in range(y_here):
        ones_here = ones_here + jnp.where(seconds[y], 1.0, 0.0)
    second_count = jnp.sum(jnp.sum(ones_here, axis=0, keepdims=True), axis=1, keepdims=True)
    slot_table = slots[...]
    mod_sum = second_count * slot_table[:, TANGENT : TANGENT + 1] + (
        float(y_here * z_here * nx) - second_count
    )
    share = jnp.where(lane_ids < strains, slot_table * mod_sum, 0.0)
    for j in range(strains):
        share = share + jnp.where(
            lane_ids == j, jnp.sum(sums[j], axis=1, keepdims=True), 0.0
        )
    partials[len(others)] = share * (1.0 / (ny * nz * nx))

    def part_copy(index):
        return pltpu.make_async_remote_copy(
            src_ref=partials.at[len(others)], dst_ref=partials.at[index],
            send_sem=part_send.at[index], recv_sem=part_recv.at[index],
            device_id=mate_id(*others[index]), device_id_type=MESH,
        )

    for index in range(len(others)):
        part_copy(index).start()
    for index in range(len(others)):
        part_copy(index).wait_recv()
    total = partials[0]
    for index in range(1, len(mates)):
        total = total + partials[index]
    totals[my_r] = total

    def total_copy(step, owner):
        return pltpu.make_async_remote_copy(
            src_ref=totals.at[my_r], dst_ref=totals.at[owner],
            send_sem=total_send.at[step], recv_sem=total_recv.at[step],
            device_id={"rve": turned(my_r, step, groups)}, device_id_type=MESH,
        )

    for step in range(1, groups):
        total_copy(step, my_r).start()
    for step in range(1, groups):
        total_copy(step, turned(my_r, -step, groups)).wait_recv()
    mine = tables[my_r]
    answer = jnp.zeros((8, 128), f32)
    for group in range(groups):
        for rank in range(CAP):
            chosen = (mine[:, TARGET : TARGET + 1] == float(group)) & (
                mine[:, RANK : RANK + 1] == float(rank)
            )
            line = totals[group, pl.ds(my_r * CAP + rank, 1), :]
            answer = answer + jnp.where(chosen, line, 0.0)
    rows_out[...] = answer[:listed, :strains]

    for step in range(1, groups):
        table_copy(step, my_r).wait_send()
        total_copy(step, my_r).wait_send()
    for index, (dy, dz) in enumerate(others):
        phase_copy(index, 0, 0).wait_send()
        force_copy(index, 0, 0).wait_send()
        part_copy(index).wait_send()
        for y in range(y_here):
            field_copy(dy, dz, y, my_load).wait_send()


def fused_body(strain, tangent, yield_list, destination, phase_map, polarization, stencil):
    groups, ngy, ngz = (lax.axis_size(name) for name in ("rve", "gy", "gz"))
    channels = polarization.shape[1]
    strains = polarization.shape[2]
    y_here, z_here, nx = polarization.shape[3:]
    ny, nz = y_here * ngy, z_here * ngz
    loads = groups * CAP
    count = ngy * ngz
    f32 = jnp.float32
    slot_rows = 3 * channels * nz
    vmem = pl.BlockSpec(memory_space=pltpu.VMEM)
    smem = pl.BlockSpec(memory_space=pltpu.SMEM)
    cell = pltpu.VMEM((ny, nz, nx), f32)
    vector = pltpu.VMEM((channels, ny, nz, nx), f32)

    def dma(*shape):
        return pltpu.SemaphoreType.DMA(shape)

    return pl.pallas_call(
        functools.partial(kernel, groups, ngy, ngz),
        out_shape=(
            jax.ShapeDtypeStruct((1, loads, channels, y_here, z_here, nx), f32),
            jax.ShapeDtypeStruct((yield_list.shape[0], strains), f32),
        ),
        in_specs=[smem, smem, smem, smem, smem, vmem, vmem],
        out_specs=(vmem, vmem),
        scratch_shapes=[
            pltpu.VMEM((groups, 8, 128), f32),
            pltpu.VMEM((loads, 128), f32),
            pltpu.VMEM((ny, nz, nx), jnp.int32),
            pltpu.VMEM((count, channels, y_here, z_here, nx), f32),
            vector,
            pltpu.VMEM((3 * channels * nz, 3 * slot_rows), jnp.bfloat16),
            pltpu.VMEM((2, (ny + 2) * slot_rows, 2 * nx), jnp.bfloat16),
            vector,
            vector,
            cell, cell, cell, cell,
            pltpu.VMEM((strains, loads, 128), f32),
            pltpu.VMEM((count, 8, 128), f32),
            pltpu.VMEM((groups, 8, 128), f32),
            dma(groups), dma(groups), dma(count), dma(count), dma(count), dma(count),
            dma(ngy, ngz, y_here), dma(ngy, ngz, y_here),
            dma(count), dma(count), dma(groups), dma(groups),
        ],
        compiler_params=pltpu.CompilerParams(
            collective_id=0, has_side_effects=True, vmem_limit_bytes=40 * 1024 * 1024
        ),
    )(strain, tangent, yield_list, destination, stencil, phase_map, polarization)


def body_for(mesh):
    def chosen(*arguments):
        strain, _, yield_list, _, phase_map, _, _ = arguments
        loads = lax.axis_size("rve") * CAP
        one_load_each = lax.axis_size("gy") * lax.axis_size("gz") == loads
        tiled = phase_map.shape[2] == 8 and phase_map.shape[3] == 128 and loads == 8
        if one_load_each and tiled and yield_list.shape[0] <= 8:
            return fused_body(*arguments)
        return body(*arguments)

    return chosen


def solution(mesh):
    return jax.shard_map(
        body_for(mesh),
        mesh=mesh,
        in_specs=(
            P("rve", None),
            P("rve"),
            P("rve"),
            P("rve", None),
            P("rve", "gy", "gz", None),
            P("rve", None, None, "gy", "gz", None),
            P(),
        ),
        out_specs=(P("rve", None, None, "gy", "gz", None), P("rve", None)),
        check_vma=False,
    )
```
